128 devices in a mesh: qr: 8 (over z_lo, x), kc: 16 (over y, z_hi, core).
Axes of the slice: x: 4, y: 4, z: 4 (z_hi: 2, z_lo: 2; z = z_hi * 2 + z_lo), core: 2. Of those that a mesh axis runs over, the one named last changes fastest.
Arguments:
- queries: bfloat16 [24576, 512], P(('qr', 'kc')), may hold values from -48 to 48, as said below
- keys: bfloat16 [24576, 512], P(('qr', 'kc')), may hold values from -16 to 16, as said below
- pair: int32 [24576], P(('qr', 'kc')), may hold values from 0 to 24575, each once
Outputs:
- loss: float32 [], replicated
- query_grad: float32 [24576, 512], P(('qr', 'kc'))
- key_grad: float32 [24576, 512], P(('qr', 'kc'))
The draws below stay inside these ranges and needn't reach their ends.
Inputs may be any that keep to these rules, and one draw needn't show every extreme that they name: queries lie within this range; the shown draw within -6 to 6. keys lie within this range; the shown draw within -6 to 6. Every key is the pair of exactly one query.
All inputs are finite; a program needn't handle non-finite values.
Results may differ from the reference program's by a relative error of at most 0.0018.
Values may be sent and summed in bfloat16 or wider, within the bound.
A program may use at most 128 MiB of HBM per device.

```python
import math
import jax
import jax.numpy as jnp
from jax import lax

E = 512
NPAIRS = 24576


def shared_base(key):
    return jax.random.truncated_normal(jax.random.fold_in(key, 11), -6.0, 6.0, (NPAIRS, E), jnp.float32)


def draw_queries(key, part):
    key = jax.random.fold_in(key, 1)
    first_key = jax.random.fold_in(key, 0)
    result = jax.random.truncated_normal(first_key, -6.0, 6.0, (NPAIRS, E), jnp.float32)
    return result.astype(jnp.bfloat16)


def draw_keys(key, part):
    shared = shared_base(key)
    result = shared
    return result.astype(jnp.bfloat16)


def setup_inputs(seed: int = 0) -> dict:
    key_list = jax.random.split(jax.random.key(seed), 4)
    queries = draw_queries(jax.random.fold_in(key_list[3], 71), 0)
    keys = draw_keys(jax.random.fold_in(key_list[3], 71), 0)
    pair = jax.random.permutation(key_list[2], NPAIRS).astype(jnp.int32)
    return {"queries": queries, "keys": keys, "pair": pair}


def reference(queries, keys, pair):
    pair_count = queries.shape[0]
    height = math.gcd(pair_count, 1024)
    blocks = jnp.arange(pair_count // height, dtype=jnp.int32)
    key_ids = jnp.arange(pair_count, dtype=jnp.int32)
    factor = 2.0 / math.sqrt(E)

    def rows_of(number):
        first_row = number * height
        query_block = lax.dynamic_slice_in_dim(queries, first_row, height, 0)
        pair_block = lax.dynamic_slice_in_dim(pair, first_row, height, 0)
        scores = jnp.dot(query_block, keys.T, preferred_element_type=jnp.float32) * factor
        positive_mask = key_ids[None, :] == pair_block[:, None]
        return (first_row, query_block, scores, positive_mask)

    def forward(state_carry, number):
        col_peak, col_mass, positive = state_carry
        first_row, query_block, scores, positive_mask = rows_of(number)
        row_peak = lax.optimization_barrier(jnp.max(scores, axis=1))
        row_lse = row_peak + jnp.log(lax.optimization_barrier(jnp.sum(jnp.exp(scores - row_peak[:, None]), axis=1)))
        new_peak = jnp.maximum(col_peak, lax.optimization_barrier(jnp.max(scores, axis=0)))
        col_mass = col_mass * jnp.exp(col_peak - new_peak) + lax.optimization_barrier(jnp.sum(jnp.exp(scores - new_peak[None, :]), axis=0))
        positive = positive + jnp.sum(jnp.where(positive_mask, scores, 0.0))
        return ((new_peak, col_mass, positive), row_lse)
    start_state = (jnp.full((pair_count,), -jnp.inf, jnp.float32), jnp.zeros((pair_count,), jnp.float32), jnp.zeros((), jnp.float32))
    (col_peak, col_mass, positive), row_lse = lax.scan(forward, start_state, blocks)
    lse_row = row_lse.reshape(pair_count)
    lse_col = col_peak + jnp.log(col_mass)
    loss = (jnp.sum(lse_row) + jnp.sum(lse_col) - 2.0 * positive) / (2.0 * pair_count)

    def backward(key_grad, number):
        first_row, query_block, scores, positive_mask = rows_of(number)
        row_part = lax.dynamic_slice_in_dim(lse_row, first_row, height, 0)
        slopes = ((jnp.exp(scores - row_part[:, None]) + jnp.exp(scores - lse_col[None, :]) - jnp.where(positive_mask, 2.0, 0.0)) * 0.5).astype(jnp.bfloat16)
        query_part = jnp.dot(slopes, keys, preferred_element_type=jnp.float32) * factor
        key_grad = key_grad + jnp.dot(slopes.T, query_block, preferred_element_type=jnp.float32) * factor
        return (key_grad, query_part)
    key_grad, query_parts = lax.scan(backward, jnp.zeros((pair_count, keys.shape[1]), jnp.float32), blocks)
    query_grad = query_parts.reshape(pair_count, keys.shape[1])
    return (loss, query_grad, key_grad)
```

```python
import functools
import math

import jax
import jax.numpy as jnp
from jax import lax
from jax.experimental import pallas as pl
from jax.experimental.pallas import tpu as pltpu
from jax.sharding import PartitionSpec as P

MESH = pl.DeviceIdType.MESH
LOG2E = math.log2(math.e)
LN2 = math.log(2.0)
QR = 8
KC = 16
B = 192
PB = 2 * B
WIDTH = 512
ROWS = KC * B
COLS = QR * B
CHUNK = 768
LANES = 128


def rows(start, size, step=16):
    return pl.ds(pl.multiple_of(start, step), size)


def nt_dot(a, b):
    return lax.dot_general(a, b, (((1,), (1,)), ((), ())), preferred_element_type=jnp.float32)


def tn_dot(a, b):
    return lax.dot_general(a, b, (((0,), (0,)), ((), ())), preferred_element_type=jnp.float32)


def kernel(
    q_ref, k_ref, pair_ref, loss_ref, qg_ref, kg_ref,
    q_all, k_all, scores, slopes, q_sum, k_sum,
    pair_own, pair_all, pair_col,
    row_send, row_recv, row_lse, col_max, col_mass, col_send, col_recv, col_lse,
    loss_a, loss_b, positive, core_recv,
    q_code, q_step, q_code_in, q_step_in, k_code, k_step, k_code_in, k_step_in,
    gather_send, gather_recv, core_send_sem, core_recv_sem,
    q_code_send, q_code_recv, q_step_send, q_step_recv, k_code_send, k_code_recv, k_step_send, k_step_recv,
    small_send, small_recv,
):
    r = lax.axis_index("qr")
    c = lax.axis_index("kc")
    zl, x = r // 4, r % 4
    y, zh, core = c // 4, (c // 2) % 2, c % 2
    factor2 = 2.0 / math.sqrt(WIDTH) * LOG2E
    factor = 2.0 / math.sqrt(WIDTH)

    def kc_dev(yy, zz, cc):
        return (r, yy * 4 + zz * 2 + cc)

    def qr_dev(zz, xx):
        return (zz * 4 + xx, c)

    def copy(src, dst, send, recv, device):
        return pltpu.make_async_remote_copy(
            src_ref=src, dst_ref=dst, send_sem=send, recv_sem=recv,
            device_id=device, device_id_type=MESH,
        )

    barrier = pltpu.get_barrier_semaphore()

    @pl.loop(1, KC)
    def _(o):
        pl.semaphore_signal(barrier, inc=1, device_id=(r, (c + o) % KC), device_id_type=MESH)

    @pl.loop(1, QR)
    def _(o):
        pl.semaphore_signal(barrier, inc=1, device_id=((r + o) % QR, c), device_id_type=MESH)

    pl.semaphore_wait(barrier, KC + QR - 2)

    yu, yd, yo = (y + 1) % 4, (y + 3) % 4, (y + 2) % 4
    xu, xd, xo = (x + 1) % 4, (x + 3) % 4, (x + 2) % 4
    zhp, zlp, corep = 1 - zh, 1 - zl, 1 - core
    H = B // 2

    def q_rows(yy, zz, cc):
        return (zz * 8 + yy * 2 + cc) * B

    def k_rows(xx, zz):
        return (zz * 4 + xx) * B

    def q_lane(yy, zz):
        return q_rows(yy, zz, core)

    q_ring = (kc_dev(yu, zh, core), kc_dev(yd, zh, core), kc_dev(y, zhp, core))
    k_ring = (qr_dev(zl, xu), qr_dev(zl, xd), qr_dev(zlp, x))

    def gather_copy(buf, base, n, start, size, device, src=None):
        view = buf.at[rows(start, size)]
        return copy(view if src is None else src, view, gather_send.at[base + n], gather_recv.at[base + n], device)

    def make_gather(buf, own, base, slot, ring, here, up, down, far, z, zp):
        to_up, to_down, to_pair = ring
        send = {
            0: gather_copy(buf, base, 0, slot(here, z), B, to_up, own),
            1: gather_copy(buf, base, 1, slot(here, z), B, to_down, own),
            2: gather_copy(buf, base, 2, slot(here, z), B, to_pair, own),
            3: gather_copy(buf, base, 3, slot(down, z), H, to_up),
            4: gather_copy(buf, base, 4, slot(up, z) + H, H, to_down),
            5: gather_copy(buf, base, 5, slot(here, zp), B, to_up),
            6: gather_copy(buf, base, 6, slot(here, zp), B, to_down),
            7: gather_copy(buf, base, 7, slot(down, zp), H, to_up),
            8: gather_copy(buf, base, 8, slot(up, zp) + H, H, to_down),
        }
        recv = {
            0: gather_copy(buf, base, 0, slot(down, z), B, to_up),
            1: gather_copy(buf, base, 1, slot(up, z), B, to_up),
            2: gather_copy(buf, base, 2, slot(here, zp), B, to_up),
            3: gather_copy(buf, base, 3, slot(far, z), H, to_up),
            4: gather_copy(buf, base, 4, slot(far, z) + H, H, to_up),
            5: gather_copy(buf, base, 5, slot(down, zp), B, to_up),
            6: gather_copy(buf, base, 6, slot(up, zp), B, to_up),
            7: gather_copy(buf, base, 7, slot(far, zp), H, to_up),
            8: gather_copy(buf, base, 8, slot(far, zp) + H, H, to_up),
        }
        return send, recv

    k_out, k_in = make_gather(k_all, k_ref, 0, k_rows, k_ring, x, xu, xd, xo, zl, zlp)
    q_out, q_in = make_gather(q_all, q_ref, 9, q_lane, q_ring, y, yu, yd, yo, zh, zhp)
    sibling = kc_dev(y, zh, corep)
    lane_slots = ((y, zh), (yd, zh), (yu, zh), (y, zhp), (yo, zh), (yd, zhp), (yu, zhp), (yo, zhp))
    swap_out = [
        gather_copy(q_all, 18, n, q_rows(yy, zz, core), B, sibling, q_ref if n == 0 else None)
        for n, (yy, zz) in enumerate(lane_slots)
    ]
    swap_in = [
        gather_copy(q_all, 18, n, q_rows(yy, zz, corep), B, sibling) for n, (yy, zz) in enumerate(lane_slots)
    ]

    for n in (0, 1, 2):
        k_out[n].start()
        q_out[n].start()
    swap_out[0].start()

    def pair_copy(o):
        return copy(pair_own, pair_all.at[c], small_send.at[o], small_recv.at[o], (r, (c + o) % KC))

    pair_own[...] = jnp.zeros((1, 2 * LANES), jnp.int32)
    pair_own[:, 0:B] = pair_ref[...]

    @pl.loop(1, KC)
    def _(o):
        pair_copy(o).start()

    q_all[rows(q_rows(y, zh, core), B), :] = q_ref[...]
    k_all[rows(k_rows(x, zl), B), :] = k_ref[...]
    pair_all[c] = pair_own[...]

    for arrived, started in ((0, (3,)), (1, (4,)), (2, (5, 6))):
        k_in[arrived].wait_recv()
        for n in started:
            k_out[n].start()
        q_in[arrived].wait_recv()
        for n in started:
            q_out[n].start()
        swap_out[arrived + 1].start()
    for n in (3, 4):
        k_in[n].wait_recv()
        q_in[n].wait_recv()
    swap_out[4].start()
    for arrived, started in ((5, 7), (6, 8)):
        k_in[arrived].wait_recv()
        k_out[started].start()
        q_in[arrived].wait_recv()
        q_out[started].start()
        swap_out[arrived].start()

    @pl.loop(1, KC)
    def _(o):
        pair_copy(o).wait_recv()

    @pl.loop(0, KC)
    def _(k):
        wide = jnp.broadcast_to(pair_all[k].astype(jnp.float32), (LANES, 2 * LANES)).T
        pair_col[rows(q_rows(k // 4, (k // 2) % 2, k % 2), B), :] = wide[:B].astype(jnp.int32)

    for n in (7, 8):
        k_in[n].wait_recv()
        q_in[n].wait_recv()
    swap_out[7].start()
    for n in range(8):
        swap_in[n].wait_recv()

    col_max[...] = jnp.full((1, COLS), -1e30, jnp.float32)
    col_mass[...] = jnp.zeros((1, COLS), jnp.float32)

    @pl.loop(0, ROWS // PB)
    def _(p):
        here = rows(p * PB, PB)
        block = q_all[here, :]
        peak = None
        for n in range(COLS // CHUNK):
            cols = pl.ds(n * CHUNK, CHUNK)
            s = nt_dot(block, k_all[cols, :]) * factor2
            scores[here, cols] = s
            top = jnp.max(s, axis=0, keepdims=True)
            mass = jnp.sum(jnp.exp2(s - top), axis=0, keepdims=True)
            old = col_max[:, cols]
            new = jnp.maximum(old, top)
            col_max[:, cols] = new
            col_mass[:, cols] = col_mass[:, cols] * jnp.exp2(old - new) + mass * jnp.exp2(top - new)
            for g in range(CHUNK // LANES):
                part = s[:, g * LANES:(g + 1) * LANES]
                peak = part if peak is None else jnp.maximum(peak, part)
        peak = jnp.broadcast_to(jnp.max(peak, axis=1, keepdims=True), (PB, LANES))
        mass = None
        for g in range(COLS // LANES):
            e = jnp.exp2(scores[here, pl.ds(g * LANES, LANES)] - peak)
            mass = e if mass is None else mass + e
        row_send[pl.ds(p, 1), :] = peak.T[0:1, :] + jnp.log(jnp.sum(mass.T, axis=0, keepdims=True)) * LOG2E

    col_send[...] = col_max[...] + jnp.log(col_mass[...]) * LOG2E

    def row_copy(o):
        return copy(row_send, row_recv.at[c], small_send.at[KC + o], small_recv.at[KC + o], (r, (c + o) % KC))

    def col_copy(o):
        return copy(col_send, col_recv.at[r], small_send.at[2 * KC + o], small_recv.at[2 * KC + o], ((r + o) % QR, c))

    @pl.loop(1, KC)
    def _(o):
        row_copy(o).start()

    @pl.loop(1, QR)
    def _(o):
        col_copy(o).start()

    row_recv[c] = row_send[...]
    col_recv[r] = col_send[...]

    def combine(recv, count):
        top = recv[0]
        for n in range(1, count):
            top = jnp.maximum(top, recv[n])
        mass = jnp.zeros_like(top)
        for n in range(count):
            mass = mass + jnp.exp2(recv[n] - top)
        return top + jnp.log(mass) * LOG2E

    @pl.loop(1, KC)
    def _(o):
        row_copy(o).wait_recv()

    row_lse[...] = combine(row_recv, KC)

    @pl.loop(1, QR)
    def _(o):
        col_copy(o).wait_recv()

    col_lse[...] = combine(col_recv, QR)

    def encode(code, step, n, value):
        unit = jnp.maximum(jnp.max(jnp.abs(value), axis=0, keepdims=True), 1e-33) * (1.0 / 32766.0)
        code[n] = jnp.round(value * (1.0 / unit)).astype(jnp.int32).astype(jnp.int16)
        step[n] = unit

    def make_reduce(buf, slot, ring, own_z, other_z, code, step, code_in, step_in, sems, here, up, down, far):
        to_up, to_down, to_pair = ring
        code_send, code_recv, step_send, step_recv = sems

        def copies(n, device):
            return (
                copy(code.at[n], code_in.at[n], code_send.at[n], code_recv.at[n], device),
                copy(step.at[n], step_in.at[n], step_send.at[n], step_recv.at[n], device),
            )

        def send(n, value, device):
            encode(code, step, n, value)
            for one in copies(n, device):
                one.start()

        def take(n):
            for one in copies(n, to_up):
                one.wait_recv()
            return code_in[n].astype(jnp.int32).astype(jnp.float32) * step_in[n]

        def half(s, place, bottom):
            return rows(slot(place, other_z if s == 0 else own_z) + (H if bottom else 0), H)

        def first(s):
            send(6 * s, buf[half(s, far, False), :], to_up)
            send(6 * s + 1, buf[half(s, far, True), :], to_down)

        def raw_up(s):
            send(6 * s + 2, buf[half(s, up, True), :], to_up)

        def raw_down(s):
            send(6 * s + 3, buf[half(s, down, False), :], to_down)

        def pass_up(s):
            send(6 * s + 4, buf[half(s, up, False), :] + take(6 * s), to_up)

        def pass_down(s):
            send(6 * s + 5, buf[half(s, down, True), :] + take(6 * s + 1), to_down)

        def final(s, bottom):
            mine = buf[half(s, here, bottom), :]
            if bottom:
                return mine + take(6 * s + 2) + take(6 * s + 5)
            return mine + take(6 * s + 3) + take(6 * s + 4)

        def pair_send():
            for n, bottom in ((12, False), (13, True)):
                send(n, final(0, bottom), to_pair)

        def result(out):
            for n, bottom in ((12, False), (13, True)):
                out[pl.ds(H if bottom else 0, H), :] = (final(1, bottom) + take(n)) * factor

        def drain():
            @pl.loop(0, 14)
            def _(n):
                for one in copies(n, to_up):
                    one.wait_send()

        return first, raw_up, raw_down, pass_up, pass_down, pair_send, result, drain

    q_first, q_raw_up, q_raw_down, q_pass_up, q_pass_down, q_pair, q_result, q_drain = make_reduce(
        q_sum, q_lane, q_ring, zh, zhp, q_code, q_step, q_code_in, q_step_in,
        (q_code_send, q_code_recv, q_step_send, q_step_recv), y, yu, yd, yo)
    k_first, k_raw_up, k_raw_down, k_pass_up, k_pass_down, k_pair, k_result, k_drain = make_reduce(
        k_sum, k_rows, k_ring, zl, zlp, k_code, k_step, k_code_in, k_step_in,
        (k_code_send, k_code_recv, k_step_send, k_step_recv), x, xu, xd, xo)

    positive[...] = jnp.zeros((8, LANES), jnp.float32)
    lane = lax.broadcasted_iota(jnp.int32, (1, LANES), 1)

    def key_ids(zz, g):
        low = (g * LANES) // B
        high = (g * LANES + LANES - 1) // B
        column = lane + (g * LANES + zz * 4 * B * KC + c * B)
        ids = column + low * (KC - 1) * B
        if low == high:
            return ids
        return jnp.where(lane + g * LANES >= high * B, column + high * (KC - 1) * B, ids)

    def step_place(t):
        return (y + jnp.where(t == 0, 2, jnp.where(t == 1, 1, jnp.where(t == 2, 3, 0)))) % 4

    def make_slopes(p, groups):
        here = rows(p * PB, PB)
        row_part = jnp.broadcast_to(row_lse[pl.ds(p, 1), :] + 1.0, (LANES, PB)).T
        pairs = pair_col[here, :]
        found = None
        for zz in groups:
            for g in range(CHUNK // LANES):
                cols = pl.ds(pl.multiple_of(zz * CHUNK + g * LANES, LANES), LANES)
                s = scores[here, cols]
                mask = key_ids(zz, g) == pairs
                z = jnp.exp2(s - row_part) + jnp.exp2(s - (col_lse[:, cols] + 1.0)) - jnp.where(mask, 1.0, 0.0)
                slopes[here, cols] = z.astype(jnp.bfloat16)
                hit = jnp.where(mask, s, 0.0)
                found = hit if found is None else found + hit
        positive[...] = positive[...] + jnp.sum(found.reshape(PB // 8, 8, LANES), axis=0)

    def core_out(zz, yy):
        n = zz * 4 + yy
        return copy(q_sum.at[rows(q_rows(yy, zz, corep), B)], core_recv.at[n], core_send_sem.at[n], core_recv_sem.at[n], sibling)

    def core_add(zz, yy):
        core_out(zz, yy).wait_recv()
        here = rows(q_lane(yy, zz), B)
        q_sum[here, :] = q_sum[here, :] + core_recv[zz * 4 + yy]

    def query_product(s, with_slopes):
        zz = zhp if s == 0 else zh

        @pl.loop(0, 4)
        def _(t):
            yy = step_place(t)
            p = zz * 4 + yy
            here = rows(p * PB, PB)
            if with_slopes:
                make_slopes(p, (0, 1))
            q_sum[here, :] = jnp.dot(slopes[here, :], k_all[...], preferred_element_type=jnp.float32)
            core_out(zz, yy).start()

            @pl.when(t > 0)
            def _():
                core_add(zz, step_place(t - 1))

            @pl.when(t == 1)
            def _():
                q_first(s)

            @pl.when(t == 2)
            def _():
                q_raw_up(s)

            @pl.when(t == 3)
            def _():
                q_raw_down(s)
                q_pass_up(s)

        core_add(zz, y)
        q_pass_down(s)

    def key_product(s):
        zz = zlp if s == 0 else zl
        cols = pl.ds(pl.multiple_of(zz * CHUNK, LANES), CHUNK)
        k_sum[rows(zz * CHUNK, CHUNK), :] = tn_dot(slopes[:, cols], q_all[...])

    def own_slopes(zz):
        @pl.loop(0, 4)
        def _(t):
            make_slopes(zh * 4 + t, (zz,))

    query_product(0, True)
    own_slopes(zlp)
    key_product(0)
    k_first(0)
    k_raw_up(0)
    k_raw_down(0)
    own_slopes(zl)

    share = jnp.sum(positive[...], axis=0, keepdims=True) * (-2.0)
    rows_lse = row_lse[pl.ds(zh * 4 + y, 1), :]
    for g in range(PB // LANES):
        share = share + jnp.where(core == 0, rows_lse[:, g * LANES:(g + 1) * LANES], 0.0)
    for g in range(CHUNK // LANES):
        cols = pl.ds(pl.multiple_of(zl * CHUNK + g * LANES, LANES), LANES)
        share = share + jnp.where(x == 0, col_lse[:, cols], 0.0)
    loss_a[c] = share

    def loss_copy_a(o):
        return copy(loss_a.at[c], loss_a.at[c], small_send.at[40 + o], small_recv.at[40 + o], (r, (c + o) % KC))

    def loss_copy_b(o):
        return copy(loss_b.at[r], loss_b.at[r], small_send.at[56 + o], small_recv.at[56 + o], ((r + o) % QR, c))

    @pl.loop(1, KC)
    def _(o):
        loss_copy_a(o).start()

    k_pass_up(0)
    k_pass_down(0)
    key_product(1)
    k_first(1)
    k_raw_up(1)
    k_raw_down(1)
    q_pair()
    query_product(1, False)
    k_pass_up(1)
    k_pass_down(1)

    @pl.loop(1, KC)
    def _(o):
        loss_copy_a(o).wait_recv()

    total = loss_a[0]
    for n in range(1, KC):
        total = total + loss_a[n]
    loss_b[r] = total

    @pl.loop(1, QR)
    def _(o):
        loss_copy_b(o).start()

    k_pair()
    q_result(qg_ref)
    k_result(kg_ref)

    @pl.loop(1, QR)
    def _(o):
        loss_copy_b(o).wait_recv()

    total = loss_b[0]
    for n in range(1, QR):
        total = total + loss_b[n]
    loss_ref[...] = jnp.sum(total, axis=1, keepdims=True) * (LN2 / (2.0 * QR * KC * B))

    for n in range(9):
        k_out[n].wait_send()
        q_out[n].wait_send()
    for n in range(8):
        swap_out[n].wait_send()

    @pl.loop(1, KC)
    def _(o):
        pair_copy(o).wait_send()
        row_copy(o).wait_send()
        loss_copy_a(o).wait_send()

    @pl.loop(1, QR)
    def _(o):
        col_copy(o).wait_send()
        loss_copy_b(o).wait_send()

    @pl.loop(0, 8)
    def _(n):
        core_out(n // 4, n % 4).wait_send()

    q_drain()
    k_drain()


def finish(loss_in, query_in, key_in, loss_ref, query_ref, key_ref):
    loss_ref[...] = loss_in[...]
    query_ref[...] = query_in[...]
    key_ref[...] = key_in[...]


def shards(queries, keys, pair):
    pair = pair.reshape(1, B)
    f32, bf16 = jnp.float32, jnp.bfloat16
    vmem = pl.BlockSpec(memory_space=pltpu.VMEM)
    dma = pltpu.SemaphoreType.DMA
    loss, query_grad, key_grad = pl.pallas_call(
        kernel,
        out_shape=(
            jax.ShapeDtypeStruct((1, 1), f32),
            jax.ShapeDtypeStruct((B, WIDTH), f32),
            jax.ShapeDtypeStruct((B, WIDTH), f32),
        ),
        in_specs=[vmem] * 3,
        out_specs=(vmem,) * 3,
        scratch_shapes=[
            pltpu.VMEM((ROWS, WIDTH), bf16),
            pltpu.VMEM((COLS, WIDTH), bf16),
            pltpu.VMEM((ROWS, COLS), f32),
            pltpu.VMEM((ROWS, COLS), bf16),
            pltpu.VMEM((ROWS, WIDTH), f32),
            pltpu.VMEM((COLS, WIDTH), f32),
            pltpu.VMEM((1, 2 * LANES), jnp.int32),
            pltpu.VMEM((KC, 1, 2 * LANES), jnp.int32),
            pltpu.VMEM((ROWS, LANES), jnp.int32),
            pltpu.VMEM((8, PB), f32),
            pltpu.VMEM((KC, 8, PB), f32),
            pltpu.VMEM((8, PB), f32),
            pltpu.VMEM((1, COLS), f32),
            pltpu.VMEM((1, COLS), f32),
            pltpu.VMEM((1, COLS), f32),
            pltpu.VMEM((QR, 1, COLS), f32),
            pltpu.VMEM((1, COLS), f32),
            pltpu.VMEM((KC, 1, LANES), f32),
            pltpu.VMEM((QR, 1, LANES), f32),
            pltpu.VMEM((8, LANES), f32),
            pltpu.VMEM((8, B, WIDTH), f32),
        ]
        + [pltpu.VMEM((14, B // 2, WIDTH), jnp.int16), pltpu.VMEM((14, 1, WIDTH), f32)] * 4
        + [dma((26,)), dma((26,)), dma((8,)), dma((8,))]
        + [dma((14,))] * 8
        + [dma((64,)), dma((64,))],
        compiler_params=pltpu.CompilerParams(
            collective_id=0, has_side_effects=True, vmem_limit_bytes=60 * 1024 * 1024
        ),
    )(queries, keys, pair)
    loss, query_grad, key_grad = pl.pallas_call(
        finish,
        out_shape=(
            jax.ShapeDtypeStruct((1, 1), f32),
            jax.ShapeDtypeStruct((B, WIDTH), f32),
            jax.ShapeDtypeStruct((B, WIDTH), f32),
        ),
        in_specs=[vmem] * 3,
        out_specs=(vmem,) * 3,
    )(loss, query_grad, key_grad)
    return loss.reshape(()), query_grad, key_grad


def solution(mesh):
    placed = (P(("qr", "kc"), None), P(("qr", "kc"), None), P(("qr", "kc")))
    return jax.shard_map(
        shards,
        mesh=mesh,
        in_specs=placed,
        out_specs=(P(), P(("qr", "kc"), None), P(("qr", "kc"), None)),
        check_vma=False,
    )
```

```python
import functools
import math

import jax
import jax.numpy as jnp
from jax import lax
from jax.experimental import pallas as pl
from jax.experimental.pallas import tpu as pltpu
from jax.sharding import PartitionSpec as P

MESH = pl.DeviceIdType.MESH
LOG2E = math.log2(math.e)
LN2 = math.log(2.0)
QR = 8
KC = 16
B = 192
PB = 2 * B
WIDTH = 512
ROWS = KC * B
COLS = QR * B
CHUNK = 768
LANES = 128
FACTOR = 2.0 / math.sqrt(WIDTH)


def rows(start, size, step=16):
    return pl.ds(pl.multiple_of(start, step), size)


def nt_dot(a, b):
    return lax.dot_general(a, b, (((1,), (1,)), ((), ())), preferred_element_type=jnp.float32)


def tn_dot(a, b):
    return lax.dot_general(a, b, (((0,), (0,)), ((), ())), preferred_element_type=jnp.float32)


def kernel(
    q_ref, k_ref, pair_ref, loss_ref, qg_ref, kg_ref,
    q_all, k_all, scores, slopes, q_sum, k_sum,
    pair_own, pair_all, pair_col,
    row_part, row_send, row_recv, row_lse, row_col, col_max, col_mass, col_send, col_recv, col_lse,
    loss_a, loss_b, positive, core_recv,
    q_code, q_step, q_code_in, q_step_in, k_code, k_step, k_code_in, k_step_in,
    own_sem, gather_send, gather_recv, core_send_sem, core_recv_sem,
    q_code_send, q_code_recv, q_step_send, q_step_recv, k_code_send, k_code_recv, k_step_send, k_step_recv,
    small_send, small_recv,
):
    r = lax.axis_index("qr")
    c = lax.axis_index("kc")
    zl, x = r // 4, r % 4
    y, zh, core = c // 4, (c // 2) % 2, c % 2
    factor2 = FACTOR * LOG2E

    def kc_dev(yy, zz, cc):
        return (r, yy * 4 + zz * 2 + cc)

    def qr_dev(zz, xx):
        return (zz * 4 + xx, c)

    def copy(src, dst, send, recv, device):
        return pltpu.make_async_remote_copy(
            src_ref=src, dst_ref=dst, send_sem=send, recv_sem=recv,
            device_id=device, device_id_type=MESH,
        )

    y, zh, core = c // 4, (c // 2) % 2, c % 2
    yu, yd, yo = (y + 1) % 4, (y + 3) % 4, (y + 2) % 4
    xu, xd, xo = (x + 1) % 4, (x + 3) % 4, (x + 2) % 4
    zhp, zlp, corep = 1 - zh, 1 - zl, 1 - core
    q_ring = (kc_dev(yu, zh, core), kc_dev(yd, zh, core), kc_dev(y, zhp, core))
    k_ring = (qr_dev(zl, xu), qr_dev(zl, xd), qr_dev(zlp, x))
    sibling = kc_dev(y, zh, corep)
    barrier = pltpu.get_barrier_semaphore()
    for near in q_ring + k_ring + (sibling,):
        pl.semaphore_signal(barrier, inc=1, device_id=near, device_id_type=MESH)
    pl.semaphore_wait(barrier, 7)

    H = B // 2

    def q_rows(yy, zz, cc):
        return (zz * 8 + yy * 2 + cc) * B

    def k_rows(xx, zz):
        return (zz * 4 + xx) * B

    def q_lane(yy, zz):
        return q_rows(yy, zz, core)

    def gather_copy(buf, n, start, size, device, src=None):
        view = buf.at[rows(start, size)]
        return copy(view if src is None else src, view, gather_send.at[n], gather_recv.at[n], device)

    def make_gather(buf, own, base, slot, ring, here, up, down, far, z, zp):
        to_up, to_down, to_pair = ring
        send, recv = {}, {}
        for h in range(2):
            half = own.at[pl.ds(h * H, H)]
            mine = slot(here, z) + h * H
            pairs = slot(here, zp) + h * H
            send[h] = gather_copy(buf, base + h, mine, H, to_up, half)
            send[2 + h] = gather_copy(buf, base + 2 + h, mine, H, to_down, half)
            send[4 + h] = gather_copy(buf, base + 4 + h, mine, H, to_pair, half)
            send[8 + h] = gather_copy(buf, base + 8 + h, pairs, H, to_up)
            send[10 + h] = gather_copy(buf, base + 10 + h, pairs, H, to_down)
            recv[h] = gather_copy(buf, base + h, slot(down, z) + h * H, H, to_up)
            recv[2 + h] = gather_copy(buf, base + 2 + h, slot(up, z) + h * H, H, to_up)
            recv[4 + h] = gather_copy(buf, base + 4 + h, pairs, H, to_up)
            recv[8 + h] = gather_copy(buf, base + 8 + h, slot(down, zp) + h * H, H, to_up)
            recv[10 + h] = gather_copy(buf, base + 10 + h, slot(up, zp) + h * H, H, to_up)
        for n, zz in ((6, z), (12, zp)):
            send[n] = gather_copy(buf, base + n, slot(down, zz), H, to_up)
            send[n + 1] = gather_copy(buf, base + n + 1, slot(up, zz) + H, H, to_down)
            recv[n] = gather_copy(buf, base + n, slot(far, zz), H, to_up)
            recv[n + 1] = gather_copy(buf, base + n + 1, slot(far, zz) + H, H, to_up)

        def start(*numbers):
            for n in numbers:
                send[n].start()

        def arrived(*numbers):
            for n in numbers:
                recv[n].wait_recv()

        def drain():
            for n in range(14):
                send[n].wait_send()

        return start, arrived, drain

    k_start, k_arrived, k_gather_drain = make_gather(k_all, k_ref, 0, k_rows, k_ring, x, xu, xd, xo, zl, zlp)
    q_start, q_arrived, q_gather_drain = make_gather(q_all, q_ref, 14, q_lane, q_ring, y, yu, yd, yo, zh, zhp)

    def ring_place(t):
        return (y + jnp.where(t == 0, 0, jnp.where(t == 1, 1, jnp.where(t == 2, 3, 2)))) % 4

    def swap_copy(s, t, cc):
        start = q_rows(ring_place(t), jnp.where(s == 0, zh, zhp), cc)
        src = q_ref if isinstance(s, int) and (s, t) == (0, 0) else None
        return gather_copy(q_all, 28 + s * 4 + t, start, B, sibling, src)

    def swap_start(s, t):
        swap_copy(s, t, core).start()

    def swap_arrived(s, t):
        swap_copy(s, t, corep).wait_recv()

    own_copies = (
        pltpu.make_async_copy(q_ref, q_all.at[rows(q_rows(y, zh, core), B)], own_sem.at[0]),
        pltpu.make_async_copy(k_ref, k_all.at[rows(k_rows(x, zl), B)], own_sem.at[1]),
    )
    k_start(4, 5)
    k_start(0, 3, 1, 2)
    q_start(0, 3, 1, 2)
    q_start(4, 5)
    swap_start(0, 0)
    for one in own_copies:
        one.start()
    pair_own[...] = jnp.zeros((1, 2 * LANES), jnp.int32)
    pair_own[:, 0:B] = pair_ref[...]
    col_max[...] = jnp.full((2, 1, CHUNK), -1e30, jnp.float32)
    col_mass[...] = jnp.zeros((2, 1, CHUNK), jnp.float32)
    for one in own_copies:
        one.wait()

    def lanes(g):
        return pl.ds(g * LANES, LANES)

    def score_unit(p, zz):
        here = rows(p * PB, PB)
        scores[zz, here, :] = nt_dot(q_all[here, :], k_all[rows(zz * CHUNK, CHUNK), :]) * factor2
        peak, tops = None, []
        for g in range(CHUNK // LANES):
            s = scores[zz, here, lanes(g)]
            peak = s if peak is None else jnp.maximum(peak, s)
            tops.append(jnp.max(s, axis=0, keepdims=True))
        peak = jnp.broadcast_to(jnp.max(peak, axis=1, keepdims=True), (PB, LANES))
        mass = None
        for g in range(CHUNK // LANES):
            s = scores[zz, here, lanes(g)]
            e = jnp.exp2(s - peak)
            mass = e if mass is None else mass + e
            new_mass = jnp.sum(jnp.exp2(s - tops[g]), axis=0, keepdims=True)
            old = col_max[zz, :, lanes(g)]
            new = jnp.maximum(old, tops[g])
            col_max[zz, :, lanes(g)] = new
            col_mass[zz, :, lanes(g)] = col_mass[zz, :, lanes(g)] * jnp.exp2(old - new) + new_mass * jnp.exp2(tops[g] - new)
        row_part[zz, pl.ds(p, 1), :] = peak.T[0:1, :] + jnp.log(jnp.sum(mass.T, axis=0, keepdims=True)) * LOG2E

    k_arrived(0)
    k_start(6)
    k_arrived(3)
    k_start(7)
    q_arrived(0)
    q_start(6)
    q_arrived(3)
    q_start(7)
    k_arrived(4)
    k_start(8, 10)
    k_arrived(1, 2)
    q_arrived(1, 2)
    swap_start(0, 1)
    swap_start(0, 2)
    k_arrived(5)
    k_start(9, 11)
    q_arrived(4)
    q_start(8, 10)
    k_arrived(6, 7)
    q_arrived(6, 7)
    swap_start(0, 3)
    swap_arrived(0, 0)

    def pair_copy(o):
        return copy(pair_own, pair_all.at[c], small_send.at[o], small_recv.at[o], (r, (c + o) % KC))

    def before_unit_1():
        k_arrived(8)
        k_start(12)
        q_arrived(5)
        q_start(9, 11)
        swap_start(1, 0)
        swap_arrived(0, 1)

    def before_unit_2():
        k_arrived(11)
        k_start(13)
        swap_arrived(0, 2)

    def before_unit_3():
        q_arrived(8)
        q_start(12)
        swap_arrived(0, 3)

    def before_unit_5():
        q_arrived(11)
        q_start(13)
        q_arrived(9, 10)
        swap_start(1, 1)
        swap_start(1, 2)
        k_arrived(9, 10, 12, 13)

    def before_unit_7():
        q_arrived(12, 13)
        swap_start(1, 3)

    def before_unit_14():
        swap_arrived(1, 3)

        @pl.loop(1, KC)
        def _(o):
            pair_copy(o).start()

    score_events = {
        1: before_unit_1, 2: before_unit_2, 3: before_unit_3, 4: lambda: swap_arrived(1, 0), 5: before_unit_5,
        7: before_unit_7, 10: lambda: swap_arrived(1, 1), 12: lambda: swap_arrived(1, 2), 14: before_unit_14,
    }

    for u in range(16):
        if u in score_events:
            score_events[u]()
        s, t, partner = (
            (0, 0, 0), (0, 1, 0), (0, 2, 0), (0, 3, 0), (1, 0, 0), (0, 0, 1), (0, 1, 1), (0, 2, 1), (0, 3, 1), (1, 0, 1),
            (1, 1, 0), (1, 1, 1), (1, 2, 0), (1, 2, 1), (1, 3, 0), (1, 3, 1),
        )[u]
        score_unit((zhp if s else zh) * 4 + ring_place(t), zlp if partner else zl)

    parts_top = jnp.maximum(row_part[0], row_part[1])
    parts_mass = jnp.exp2(row_part[0] - parts_top) + jnp.exp2(row_part[1] - parts_top)
    row_send[...] = parts_top + jnp.log(parts_mass) * LOG2E
    col_send[...] = col_max[...] + jnp.log(col_mass[...]) * LOG2E

    def row_copy(o):
        return copy(row_send, row_recv.at[c], small_send.at[KC + o], small_recv.at[KC + o], (r, (c + o) % KC))

    def col_copy(o):
        return copy(col_send, col_recv.at[r], small_send.at[2 * KC + o], small_recv.at[2 * KC + o], ((r + o) % QR, c))

    @pl.loop(1, KC)
    def _(o):
        row_copy(o).start()

    @pl.loop(1, QR)
    def _(o):
        col_copy(o).start()

    row_recv[c] = row_send[...]
    col_recv[r] = col_send[...]
    pair_all[c] = pair_own[...]

    @pl.loop(1, KC)
    def _(o):
        pair_copy(o).wait_recv()

    @pl.loop(0, KC)
    def _(k):
        wide = jnp.broadcast_to(pair_all[k].astype(jnp.float32), (LANES, 2 * LANES)).T
        pair_col[rows(q_rows(k // 4, (k // 2) % 2, k % 2), B), :] = wide[:B].astype(jnp.int32)

    def combine(recv, count):
        top = recv[0]
        for n in range(1, count):
            top = jnp.maximum(top, recv[n])
        mass = jnp.zeros_like(top)
        for n in range(count):
            mass = mass + jnp.exp2(recv[n] - top)
        return top + jnp.log(mass) * LOG2E

    @pl.loop(1, KC)
    def _(o):
        row_copy(o).wait_recv()

    row_lse[...] = combine(row_recv, KC)

    @pl.loop(0, 8)
    def _(p):
        row_col[rows(p * PB, PB), :] = jnp.broadcast_to(row_lse[pl.ds(p, 1), :] + 1.0, (LANES, PB)).T

    @pl.loop(1, QR)
    def _(o):
        col_copy(o).wait_recv()

    col_lse[...] = combine(col_recv, QR)

    def encode(code, step, n, value):
        unit = jnp.maximum(jnp.max(jnp.abs(value), axis=0, keepdims=True), 1e-33) * (1.0 / 32766.0)
        code[n] = jnp.round(value * (1.0 / unit)).astype(jnp.int32).astype(jnp.int16)
        step[n] = unit

    def make_reduce(buf, slot, ring, own_z, other_z, code, step, code_in, step_in, sems, here, up, down, far):
        to_up, to_down, to_pair = ring
        code_send, code_recv, step_send, step_recv = sems

        def copies(n, device):
            return (
                copy(code.at[n], code_in.at[n], code_send.at[n], code_recv.at[n], device),
                copy(step.at[n], step_in.at[n], step_send.at[n], step_recv.at[n], device),
            )

        def send(n, value, device):
            encode(code, step, n, value)
            for one in copies(n, device):
                one.start()

        def take(n):
            for one in copies(n, to_up):
                one.wait_recv()
            return code_in[n].astype(jnp.int32).astype(jnp.float32) * step_in[n]

        def half(s, place, bottom):
            return rows(slot(place, other_z if s == 0 else own_z) + (H if bottom else 0), H)

        def first(s):
            send(6 * s, buf[half(s, far, False), :], to_up)
            send(6 * s + 1, buf[half(s, far, True), :], to_down)

        def raw_up(s):
            send(6 * s + 2, buf[half(s, up, True), :], to_up)

        def raw_down(s):
            send(6 * s + 3, buf[half(s, down, False), :], to_down)

        def pass_up(s):
            send(6 * s + 4, buf[half(s, up, False), :] + take(6 * s), to_up)

        def pass_down(s):
            send(6 * s + 5, buf[half(s, down, True), :] + take(6 * s + 1), to_down)

        def final(s, bottom):
            mine = buf[half(s, here, bottom), :]
            if bottom:
                return mine + take(6 * s + 2) + take(6 * s + 5)
            return mine + take(6 * s + 3) + take(6 * s + 4)

        def pair_send():
            for n, bottom in ((12, False), (13, True)):
                send(n, final(0, bottom), to_pair)

        def result(out):
            for n, bottom in ((12, False), (13, True)):
                out[pl.ds(H if bottom else 0, H), :] = final(1, bottom) + take(n)

        def drain():
            @pl.loop(0, 14)
            def _(n):
                for one in copies(n, to_up):
                    one.wait_send()

        return first, raw_up, raw_down, pass_up, pass_down, pair_send, result, drain

    q_first, q_raw_up, q_raw_down, q_pass_up, q_pass_down, q_pair, q_result, q_drain = make_reduce(
        q_sum, q_lane, q_ring, zh, zhp, q_code, q_step, q_code_in, q_step_in,
        (q_code_send, q_code_recv, q_step_send, q_step_recv), y, yu, yd, yo)
    k_first, k_raw_up, k_raw_down, k_pass_up, k_pass_down, k_pair, k_result, k_drain = make_reduce(
        k_sum, k_rows, k_ring, zl, zlp, k_code, k_step, k_code_in, k_step_in,
        (k_code_send, k_code_recv, k_step_send, k_step_recv), x, xu, xd, xo)

    positive[...] = jnp.zeros((8, LANES), jnp.float32)
    lane = lax.broadcasted_iota(jnp.int32, (1, LANES), 1)

    def key_ids(zz, g):
        low = (g * LANES) // B
        high = (g * LANES + LANES - 1) // B
        column = lane + (g * LANES + zz * 4 * B * KC + c * B)
        ids = column + low * (KC - 1) * B
        if low == high:
            return ids
        return jnp.where(lane + g * LANES >= high * B, column + high * (KC - 1) * B, ids)

    def step_place(t):
        return (y + jnp.where(t == 0, 2, jnp.where(t == 1, 1, jnp.where(t == 2, 3, 0)))) % 4

    strip = LANES

    def make_slopes(p, zz):
        @pl.loop(0, PB // strip)
        def _(i):
            here = rows(p * PB + i * strip, strip)
            peak = row_col[here, :]
            pairs = pair_col[here, :]
            found = jnp.zeros((8, LANES), jnp.float32)
            for g in range(CHUNK // LANES):
                s = scores[zz, here, lanes(g)]
                mask = key_ids(zz, g) == pairs
                z = jnp.exp2(s - peak) + jnp.exp2(s - (col_lse[zz, :, lanes(g)] + 1.0)) - jnp.where(mask, 1.0, 0.0)
                slopes[zz, here, lanes(g)] = z.astype(jnp.bfloat16)
                found = found + jnp.sum(jnp.where(mask, s, 0.0).reshape(strip // 8, 8, LANES), axis=0)
            positive[...] = positive[...] + found

    def core_out(zz, yy):
        n = zz * 4 + yy
        return copy(q_sum.at[rows(q_rows(yy, zz, corep), B)], core_recv.at[n], core_send_sem.at[n], core_recv_sem.at[n], sibling)

    def core_add(zz, yy):
        core_out(zz, yy).wait_recv()
        here = rows(q_lane(yy, zz), B)
        q_sum[here, :] = q_sum[here, :] + core_recv[zz * 4 + yy]

    def tile_place(k):
        return (zhp + k // 4) % 2, step_place(k % 4)

    def slope_unit(u):
        k = jnp.where(u == 0, 0, jnp.where(u < 9, u - 1, u - 8))
        zz, yy = tile_place(k)
        make_slopes(zz * 4 + yy, (zl + jnp.where((u >= 1) & (u < 9), 1, 0)) % 2)

    def add_tile(k):
        core_add(*tile_place(k))

    def slope_units(low, high):
        @pl.loop(low, high)
        def _(u):
            slope_unit(u)

    def query_tile(k):
        zz, yy = tile_place(k)
        here = rows((zz * 4 + yy) * PB, PB)
        q_sum[here, :] = (
            jnp.dot(slopes[0, here, :], k_all[pl.ds(0, CHUNK), :], preferred_element_type=jnp.float32)
            + jnp.dot(slopes[1, here, :], k_all[pl.ds(CHUNK, CHUNK), :], preferred_element_type=jnp.float32)
        )
        core_out(zz, yy).start()

    def key_tile(zz, half):
        cols = pl.ds(pl.multiple_of(half * PB, LANES), PB)
        k_sum[rows(zz * CHUNK + half * PB, PB), :] = tn_dot(slopes[zz, :, cols], q_all[...])

    far_half, near_half = 1 - x // 2, x // 2
    slope_units(0, 2)
    query_tile(0)
    slope_units(2, 9)
    add_tile(0)
    q_first(0)
    key_tile(zlp, far_half)
    k_first(0)
    slope_units(9, 10)
    query_tile(1)
    slope_units(10, 11)
    query_tile(2)
    add_tile(1)
    q_raw_up(0)
    key_tile(zlp, near_half)
    k_raw_up(0)
    k_raw_down(0)
    add_tile(2)
    q_raw_down(0)
    slope_units(11, 16)
    share = jnp.sum(positive[...], axis=0, keepdims=True) * (-2.0)
    rows_lse = row_lse[pl.ds(zh * 4 + y, 1), :]
    for g in range(PB // LANES):
        share = share + jnp.where(core == 0, rows_lse[:, g * LANES:(g + 1) * LANES], 0.0)
    for g in range(CHUNK // LANES):
        share = share + jnp.where(x == 0, col_lse[zl, :, lanes(g)], 0.0)
    loss_a[c] = share

    def loss_copy_a(o):
        return copy(loss_a.at[c], loss_a.at[c], small_send.at[40 + o], small_recv.at[40 + o], (r, (c + o) % KC))

    def loss_copy_b(o):
        return copy(loss_b.at[r], loss_b.at[r], small_send.at[56 + o], small_recv.at[56 + o], ((r + o) % QR, c))

    @pl.loop(1, KC)
    def _(o):
        loss_copy_a(o).start()

    q_pass_up(0)
    q_pass_down(0)
    query_tile(4)
    k_pass_up(0)
    k_pass_down(0)
    key_tile(zl, far_half)
    add_tile(4)
    q_first(1)
    k_first(1)
    query_tile(3)
    query_tile(5)
    add_tile(3)
    query_tile(6)
    add_tile(5)
    q_raw_up(1)
    key_tile(zl, near_half)
    k_raw_up(1)
    k_raw_down(1)
    @pl.loop(1, KC)
    def _(o):
        loss_copy_a(o).wait_recv()

    total = loss_a[0]
    for n in range(1, KC):
        total = total + loss_a[n]
    loss_b[r] = total

    @pl.loop(1, QR)
    def _(o):
        loss_copy_b(o).start()

    add_tile(6)
    q_raw_down(1)
    q_pair()
    query_tile(7)
    k_pair()

    q_pass_up(1)
    q_pass_down(1)
    k_pass_up(1)
    k_pass_down(1)
    add_tile(7)

    k_result(kg_ref)
    q_result(qg_ref)

    @pl.loop(1, QR)
    def _(o):
        loss_copy_b(o).wait_recv()

    total = loss_b[0]
    for n in range(1, QR):
        total = total + loss_b[n]
    loss_ref[...] = jnp.sum(total, axis=1, keepdims=True) * (LN2 / (2.0 * QR * KC * B))

    k_gather_drain()
    q_gather_drain()
    for s in range(2):
        for t in range(4):
            swap_copy(s, t, core).wait_send()

    @pl.loop(1, KC)
    def _(o):
        pair_copy(o).wait_send()
        row_copy(o).wait_send()
        loss_copy_a(o).wait_send()

    @pl.loop(1, QR)
    def _(o):
        col_copy(o).wait_send()
        loss_copy_b(o).wait_send()

    @pl.loop(0, 8)
    def _(n):
        core_out(n // 4, n % 4).wait_send()

    q_drain()
    k_drain()


def finish(loss_in, query_in, key_in, loss_ref, query_ref, key_ref):
    loss_ref[...] = loss_in[...]
    query_ref[...] = query_in[...] * FACTOR
    key_ref[...] = key_in[...] * FACTOR


def shards(queries, keys, pair):
    pair = pair.reshape(1, B)
    f32, bf16 = jnp.float32, jnp.bfloat16
    vmem = pl.BlockSpec(memory_space=pltpu.VMEM)
    dma = pltpu.SemaphoreType.DMA
    loss, query_grad, key_grad = pl.pallas_call(
        kernel,
        out_shape=(
            jax.ShapeDtypeStruct((1, 1), f32),
            jax.ShapeDtypeStruct((B, WIDTH), f32),
            jax.ShapeDtypeStruct((B, WIDTH), f32),
        ),
        in_specs=[pl.BlockSpec(memory_space=pl.ANY)] * 2 + [vmem],
        out_specs=(vmem,) * 3,
        scratch_shapes=[
            pltpu.VMEM((ROWS, WIDTH), bf16),
            pltpu.VMEM((COLS, WIDTH), bf16),
            pltpu.VMEM((2, ROWS, CHUNK), f32),
            pltpu.VMEM((2, ROWS, CHUNK), bf16),
            pltpu.VMEM((ROWS, WIDTH), f32),
            pltpu.VMEM((COLS, WIDTH), f32),
            pltpu.VMEM((1, 2 * LANES), jnp.int32),
            pltpu.VMEM((KC, 1, 2 * LANES), jnp.int32),
            pltpu.VMEM((ROWS, LANES), jnp.int32),
            pltpu.VMEM((2, 8, PB), f32),
            pltpu.VMEM((8, PB), f32),
            pltpu.VMEM((KC, 8, PB), f32),
            pltpu.VMEM((8, PB), f32),
            pltpu.VMEM((ROWS, LANES), f32),
            pltpu.VMEM((2, 1, CHUNK), f32),
            pltpu.VMEM((2, 1, CHUNK), f32),
            pltpu.VMEM((2, 1, CHUNK), f32),
            pltpu.VMEM((QR, 2, 1, CHUNK), f32),
            pltpu.VMEM((2, 1, CHUNK), f32),
            pltpu.VMEM((KC, 1, LANES), f32),
            pltpu.VMEM((QR, 1, LANES), f32),
            pltpu.VMEM((8, LANES), f32),
            pltpu.VMEM((8, B, WIDTH), f32),
        ]
        + [pltpu.VMEM((14, B // 2, WIDTH), jnp.int16), pltpu.VMEM((14, 1, WIDTH), f32)] * 4
        + [dma((2,)), dma((36,)), dma((36,)), dma((8,)), dma((8,))]
        + [dma((14,))] * 8
        + [dma((64,)), dma((64,))],
        compiler_params=pltpu.CompilerParams(
            collective_id=0, has_side_effects=True, vmem_limit_bytes=60 * 1024 * 1024
        ),
    )(queries, keys, pair)
    loss, query_grad, key_grad = pl.pallas_call(
        finish,
        out_shape=(
            jax.ShapeDtypeStruct((1, 1), f32),
            jax.ShapeDtypeStruct((B, WIDTH), f32),
            jax.ShapeDtypeStruct((B, WIDTH), f32),
        ),
        in_specs=[vmem] * 3,
        out_specs=(vmem,) * 3,
    )(loss, query_grad, key_grad)
    return loss.reshape(()), query_grad, key_grad


def solution(mesh):
    placed = (P(("qr", "kc"), None), P(("qr", "kc"), None), P(("qr", "kc")))
    return jax.shard_map(
        shards,
        mesh=mesh,
        in_specs=placed,
        out_specs=(P(), P(("qr", "kc"), None), P(("qr", "kc"), None)),
        check_vma=False,
    )
```

```python
import functools
import math

import jax
import jax.numpy as jnp
from jax import lax
from jax.experimental import pallas as pl
from jax.experimental.pallas import tpu as pltpu
from jax.sharding import PartitionSpec as P

MESH = pl.DeviceIdType.MESH
LOG2E = math.log2(math.e)
LN2 = math.log(2.0)
QR = 8
KC = 16
B = 192
PB = 2 * B
WIDTH = 512
ROWS = KC * B
COLS = QR * B
CHUNK = 768
LANES = 128
FACTOR = 2.0 / math.sqrt(WIDTH)


def rows(start, size, step=16):
    return pl.ds(pl.multiple_of(start, step), size)


def nt_dot(a, b):
    return lax.dot_general(a, b, (((1,), (1,)), ((), ())), preferred_element_type=jnp.float32)


def tn_dot(a, b):
    return lax.dot_general(a, b, (((0,), (0,)), ((), ())), preferred_element_type=jnp.float32)


def kernel(
    q_ref, k_ref, pair_ref, loss_ref, qg_ref, kg_ref,
    q_all, k_all, scores, slopes, q_sum, k_sum,
    pair_own, pair_all, pair_col,
    row_part, row_send, row_recv, row_lse, row_col, col_max, col_mass, col_send, col_recv, col_lse,
    loss_a, loss_b, positive, core_recv,
    q_code, q_step, q_code_in, q_step_in, k_code, k_step, k_code_in, k_step_in,
    own_sem, gather_send, gather_recv, core_send_sem, core_recv_sem,
    q_code_send, q_code_recv, q_step_send, q_step_recv, k_code_send, k_code_recv, k_step_send, k_step_recv,
    small_send, small_recv,
):
    r = lax.axis_index("qr")
    c = lax.axis_index("kc")
    zl, x = r // 4, r % 4
    y, zh, core = c // 4, (c // 2) % 2, c % 2
    factor2 = FACTOR * LOG2E

    def kc_dev(yy, zz, cc):
        return (r, yy * 4 + zz * 2 + cc)

    def qr_dev(zz, xx):
        return (zz * 4 + xx, c)

    def copy(src, dst, send, recv, device):
        return pltpu.make_async_remote_copy(
            src_ref=src, dst_ref=dst, send_sem=send, recv_sem=recv,
            device_id=device, device_id_type=MESH,
        )

    y, zh, core = c // 4, (c // 2) % 2, c % 2
    yu, yd, yo = (y + 1) % 4, (y + 3) % 4, (y + 2) % 4
    xu, xd, xo = (x + 1) % 4, (x + 3) % 4, (x + 2) % 4
    zhp, zlp, corep = 1 - zh, 1 - zl, 1 - core
    q_ring = (kc_dev(yu, zh, core), kc_dev(yd, zh, core), kc_dev(y, zhp, core))
    k_ring = (qr_dev(zl, xu), qr_dev(zl, xd), qr_dev(zlp, x))
    sibling = kc_dev(y, zh, corep)
    barrier = pltpu.get_barrier_semaphore()
    for near in q_ring + k_ring + (sibling,):
        pl.semaphore_signal(barrier, inc=1, device_id=near, device_id_type=MESH)
    pl.semaphore_wait(barrier, 7)

    H = B // 2

    def q_rows(yy, zz, cc):
        return (zz * 8 + yy * 2 + cc) * B

    def k_rows(xx, zz):
        return (zz * 4 + xx) * B

    def q_lane(yy, zz):
        return q_rows(yy, zz, core)

    def gather_copy(buf, n, start, size, device, src=None):
        view = buf.at[rows(start, size)]
        return copy(view if src is None else src, view, gather_send.at[n], gather_recv.at[n], device)

    def make_gather(buf, own, base, slot, ring, here, up, down, far, z, zp):
        to_up, to_down, to_pair = ring
        send, recv = {}, {}
        for h in range(2):
            half = own.at[pl.ds(h * H, H)]
            mine = slot(here, z) + h * H
            pairs = slot(here, zp) + h * H
            send[h] = gather_copy(buf, base + h, mine, H, to_up, half)
            send[2 + h] = gather_copy(buf, base + 2 + h, mine, H, to_down, half)
            send[4 + h] = gather_copy(buf, base + 4 + h, mine, H, to_pair, half)
            send[8 + h] = gather_copy(buf, base + 8 + h, pairs, H, to_up)
            send[10 + h] = gather_copy(buf, base + 10 + h, pairs, H, to_down)
            recv[h] = gather_copy(buf, base + h, slot(down, z) + h * H, H, to_up)
            recv[2 + h] = gather_copy(buf, base + 2 + h, slot(up, z) + h * H, H, to_up)
            recv[4 + h] = gather_copy(buf, base + 4 + h, pairs, H, to_up)
            recv[8 + h] = gather_copy(buf, base + 8 + h, slot(down, zp) + h * H, H, to_up)
            recv[10 + h] = gather_copy(buf, base + 10 + h, slot(up, zp) + h * H, H, to_up)
        for n, zz in ((6, z), (12, zp)):
            send[n] = gather_copy(buf, base + n, slot(down, zz), H, to_up)
            send[n + 1] = gather_copy(buf, base + n + 1, slot(up, zz) + H, H, to_down)
            recv[n] = gather_copy(buf, base + n, slot(far, zz), H, to_up)
            recv[n + 1] = gather_copy(buf, base + n + 1, slot(far, zz) + H, H, to_up)

        def start(*numbers):
            for n in numbers:
                send[n].start()

        def arrived(*numbers):
            for n in numbers:
                recv[n].wait_recv()

        def drain():
            for n in range(14):
                send[n].wait_send()

        return start, arrived, drain

    k_start, k_arrived, k_gather_drain = make_gather(k_all, k_ref, 0, k_rows, k_ring, x, xu, xd, xo, zl, zlp)
    q_start, q_arrived, q_gather_drain = make_gather(q_all, q_ref, 14, q_lane, q_ring, y, yu, yd, yo, zh, zhp)

    def ring_place(t):
        return (y + jnp.where(t == 0, 0, jnp.where(t == 1, 1, jnp.where(t == 2, 3, 2)))) % 4

    def swap_copy(s, t, cc):
        start = q_rows(ring_place(t), jnp.where(s == 0, zh, zhp), cc)
        src = q_ref if isinstance(s, int) and (s, t) == (0, 0) else None
        return gather_copy(q_all, 28 + s * 4 + t, start, B, sibling, src)

    def swap_start(s, t):
        swap_copy(s, t, core).start()

    def swap_arrived(s, t):
        swap_copy(s, t, corep).wait_recv()

    own_copies = (
        pltpu.make_async_copy(q_ref, q_all.at[rows(q_rows(y, zh, core), B)], own_sem.at[0]),
        pltpu.make_async_copy(k_ref, k_all.at[rows(k_rows(x, zl), B)], own_sem.at[1]),
    )
    k_start(4, 5)
    k_start(0, 3, 1, 2)
    q_start(0, 3, 1, 2)
    q_start(4, 5)
    swap_start(0, 0)
    for one in own_copies:
        one.start()
    pair_own[...] = jnp.zeros((1, 2 * LANES), jnp.int32)
    pair_own[:, 0:B] = pair_ref[...]
    col_max[...] = jnp.full((2, 1, CHUNK), -1e30, jnp.float32)
    col_mass[...] = jnp.zeros((2, 1, CHUNK), jnp.float32)
    for one in own_copies:
        one.wait()

    def lanes(g):
        return pl.ds(g * LANES, LANES)

    def score_unit(p, zz):
        here = rows(p * PB, PB)
        scores[zz, here, :] = nt_dot(q_all[here, :], k_all[rows(zz * CHUNK, CHUNK), :]) * factor2
        peak, tops = None, []
        for g in range(CHUNK // LANES):
            s = scores[zz, here, lanes(g)]
            peak = s if peak is None else jnp.maximum(peak, s)
            tops.append(jnp.max(s, axis=0, keepdims=True))
        peak = jnp.broadcast_to(jnp.max(peak, axis=1, keepdims=True), (PB, LANES))
        mass = None
        for g in range(CHUNK // LANES):
            s = scores[zz, here, lanes(g)]
            e = jnp.exp2(s - peak)
            mass = e if mass is None else mass + e
            new_mass = jnp.sum(jnp.exp2(s - tops[g]), axis=0, keepdims=True)
            old = col_max[zz, :, lanes(g)]
            new = jnp.maximum(old, tops[g])
            col_max[zz, :, lanes(g)] = new
            col_mass[zz, :, lanes(g)] = col_mass[zz, :, lanes(g)] * jnp.exp2(old - new) + new_mass * jnp.exp2(tops[g] - new)
        row_part[zz, pl.ds(p, 1), :] = peak.T[0:1, :] + jnp.log(jnp.sum(mass.T, axis=0, keepdims=True)) * LOG2E

    k_arrived(0)
    k_start(6)
    k_arrived(3)
    k_start(7)
    q_arrived(0)
    q_start(6)
    q_arrived(3)
    q_start(7)
    k_arrived(4)
    k_start(8, 10)
    k_arrived(1, 2)
    q_arrived(1, 2)
    swap_start(0, 1)
    swap_start(0, 2)
    k_arrived(5)
    k_start(9, 11)
    q_arrived(4)
    q_start(8, 10)
    k_arrived(6, 7)
    q_arrived(6, 7)
    swap_start(0, 3)
    swap_arrived(0, 0)

    def pair_copy(o):
        return copy(pair_own, pair_all.at[c], small_send.at[o], small_recv.at[o], (r, (c + o) % KC))

    def before_unit_1():
        k_arrived(8)
        k_start(12)
        q_arrived(5)
        q_start(9, 11)
        swap_start(1, 0)
        swap_arrived(0, 1)

    def before_unit_2():
        k_arrived(11)
        k_start(13)
        swap_arrived(0, 2)

    def before_unit_3():
        q_arrived(8)
        q_start(12)
        swap_arrived(0, 3)

    def before_unit_5():
        q_arrived(11)
        q_start(13)
        q_arrived(9, 10)
        swap_start(1, 1)
        swap_start(1, 2)
        k_arrived(9, 10, 12, 13)

    def before_unit_7():
        q_arrived(12, 13)
        swap_start(1, 3)

    def before_unit_14():
        swap_arrived(1, 3)

        @pl.loop(1, KC)
        def _(o):
            pair_copy(o).start()

    score_events = {
        1: before_unit_1, 2: before_unit_2, 3: before_unit_3, 4: lambda: swap_arrived(1, 0), 5: before_unit_5,
        7: before_unit_7, 10: lambda: swap_arrived(1, 1), 12: lambda: swap_arrived(1, 2), 14: before_unit_14,
    }

    for u in range(16):
        if u in score_events:
            score_events[u]()
        s, t, partner = (
            (0, 0, 0), (0, 1, 0), (0, 2, 0), (0, 3, 0), (1, 0, 0), (0, 0, 1), (0, 1, 1), (0, 2, 1), (0, 3, 1), (1, 0, 1),
            (1, 1, 0), (1, 1, 1), (1, 2, 0), (1, 2, 1), (1, 3, 0), (1, 3, 1),
        )[u]
        score_unit((zhp if s else zh) * 4 + ring_place(t), zlp if partner else zl)

    parts_top = jnp.maximum(row_part[0], row_part[1])
    parts_mass = jnp.exp2(row_part[0] - parts_top) + jnp.exp2(row_part[1] - parts_top)
    row_send[...] = parts_top + jnp.log(parts_mass) * LOG2E
    col_send[...] = col_max[...] + jnp.log(col_mass[...]) * LOG2E

    def row_copy(o):
        return copy(row_send, row_recv.at[c], small_send.at[KC + o], small_recv.at[KC + o], (r, (c + o) % KC))

    def col_copy(o):
        return copy(col_send, col_recv.at[r], small_send.at[2 * KC + o], small_recv.at[2 * KC + o], ((r + o) % QR, c))

    @pl.loop(1, KC)
    def _(o):
        row_copy(o).start()

    @pl.loop(1, QR)
    def _(o):
        col_copy(o).start()

    row_recv[c] = row_send[...]
    col_recv[r] = col_send[...]
    pair_all[c] = pair_own[...]

    @pl.loop(1, KC)
    def _(o):
        pair_copy(o).wait_recv()

    @pl.loop(0, KC)
    def _(k):
        wide = jnp.broadcast_to(pair_all[k].astype(jnp.float32), (LANES, 2 * LANES)).T
        pair_col[rows(q_rows(k // 4, (k // 2) % 2, k % 2), B), :] = wide[:B].astype(jnp.int32)

    def combine(recv, count):
        top = recv[0]
        for n in range(1, count):
            top = jnp.maximum(top, recv[n])
        mass = jnp.zeros_like(top)
        for n in range(count):
            mass = mass + jnp.exp2(recv[n] - top)
        return top + jnp.log(mass) * LOG2E

    @pl.loop(1, KC)
    def _(o):
        row_copy(o).wait_recv()

    row_lse[...] = combine(row_recv, KC)

    @pl.loop(0, 8)
    def _(p):
        row_col[rows(p * PB, PB), :] = jnp.broadcast_to(row_lse[pl.ds(p, 1), :] + 1.0, (LANES, PB)).T

    @pl.loop(1, QR)
    def _(o):
        col_copy(o).wait_recv()

    col_lse[...] = combine(col_recv, QR)

    def encode(code, step, n, value):
        unit = jnp.maximum(jnp.max(jnp.abs(value), axis=0, keepdims=True), 1e-33) * (1.0 / 32766.0)
        code[n] = jnp.round(value * (1.0 / unit)).astype(jnp.int32).astype(jnp.int16)
        step[n] = unit

    def make_reduce(buf, slot, ring, own_z, other_z, code, step, code_in, step_in, sems, here, up, down, far):
        to_up, to_down, to_pair = ring
        code_send, code_recv, step_send, step_recv = sems

        def copies(n, device):
            return (
                copy(code.at[n], code_in.at[n], code_send.at[n], code_recv.at[n], device),
                copy(step.at[n], step_in.at[n], step_send.at[n], step_recv.at[n], device),
            )

        def send(n, value, device):
            encode(code, step, n, value)
            for one in copies(n, device):
                one.start()

        def take(n):
            for one in copies(n, to_up):
                one.wait_recv()
            return code_in[n].astype(jnp.int32).astype(jnp.float32) * step_in[n]

        def half(s, place, bottom):
            return rows(slot(place, other_z if s == 0 else own_z) + (H if bottom else 0), H)

        def first(s):
            send(6 * s, buf[half(s, far, False), :], to_up)
            send(6 * s + 1, buf[half(s, far, True), :], to_down)

        def raw_up(s):
            send(6 * s + 2, buf[half(s, up, True), :], to_up)

        def raw_down(s):
            send(6 * s + 3, buf[half(s, down, False), :], to_down)

        def pass_up(s):
            send(6 * s + 4, buf[half(s, up, False), :] + take(6 * s), to_up)

        def pass_down(s):
            send(6 * s + 5, buf[half(s, down, True), :] + take(6 * s + 1), to_down)

        def final(s, bottom):
            mine = buf[half(s, here, bottom), :]
            if bottom:
                return mine + take(6 * s + 2) + take(6 * s + 5)
            return mine + take(6 * s + 3) + take(6 * s + 4)

        def pair_send():
            for n, bottom in ((12, False), (13, True)):
                send(n, final(0, bottom), to_pair)

        def result(out):
            for n, bottom in ((12, False), (13, True)):
                out[pl.ds(H if bottom else 0, H), :] = final(1, bottom) + take(n)

        def drain():
            @pl.loop(0, 14)
            def _(n):
                for one in copies(n, to_up):
                    one.wait_send()

        return first, raw_up, raw_down, pass_up, pass_down, pair_send, result, drain

    q_first, q_raw_up, q_raw_down, q_pass_up, q_pass_down, q_pair, q_result, q_drain = make_reduce(
        q_sum, q_lane, q_ring, zh, zhp, q_code, q_step, q_code_in, q_step_in,
        (q_code_send, q_code_recv, q_step_send, q_step_recv), y, yu, yd, yo)
    k_first, k_raw_up, k_raw_down, k_pass_up, k_pass_down, k_pair, k_result, k_drain = make_reduce(
        k_sum, k_rows, k_ring, zl, zlp, k_code, k_step, k_code_in, k_step_in,
        (k_code_send, k_code_recv, k_step_send, k_step_recv), x, xu, xd, xo)

    positive[...] = jnp.zeros((8, LANES), jnp.float32)
    lane = lax.broadcasted_iota(jnp.int32, (1, LANES), 1)

    def key_ids(zz, g):
        low = (g * LANES) // B
        high = (g * LANES + LANES - 1) // B
        column = lane + (g * LANES + zz * 4 * B * KC + c * B)
        ids = column + low * (KC - 1) * B
        if low == high:
            return ids
        return jnp.where(lane + g * LANES >= high * B, column + high * (KC - 1) * B, ids)

    def step_place(t):
        return (y + jnp.where(t == 0, 2, jnp.where(t == 1, 1, jnp.where(t == 2, 3, 0)))) % 4

    strip = PB

    def make_slopes(p, zz):
        @pl.loop(0, PB // strip)
        def _(i):
            here = rows(p * PB + i * strip, strip)
            peak = row_col[here, :]
            pairs = pair_col[here, :]
            found = jnp.zeros((8, LANES), jnp.float32)
            for g in range(CHUNK // LANES):
                s = scores[zz, here, lanes(g)]
                mask = key_ids(zz, g) == pairs
                z = jnp.exp2(s - peak) + jnp.exp2(s - (col_lse[zz, :, lanes(g)] + 1.0)) - jnp.where(mask, 1.0, 0.0)
                slopes[zz, here, lanes(g)] = z.astype(jnp.bfloat16)
                found = found + jnp.sum(jnp.where(mask, s, 0.0).reshape(strip // 8, 8, LANES), axis=0)
            positive[...] = positive[...] + found

    def core_out(zz, yy):
        n = zz * 4 + yy
        return copy(q_sum.at[rows(q_rows(yy, zz, corep), B)], core_recv.at[n], core_send_sem.at[n], core_recv_sem.at[n], sibling)

    def core_add(zz, yy):
        core_out(zz, yy).wait_recv()
        here = rows(q_lane(yy, zz), B)
        q_sum[here, :] = q_sum[here, :] + core_recv[zz * 4 + yy]

    def tile_place(k):
        return (zhp + k // 4) % 2, step_place(k % 4)

    def slope_unit(u):
        k = jnp.where(u == 0, 0, jnp.where(u < 9, u - 1, u - 8))
        zz, yy = tile_place(k)
        make_slopes(zz * 4 + yy, (zl + jnp.where((u >= 1) & (u < 9), 1, 0)) % 2)

    def add_tile(k):
        core_add(*tile_place(k))

    def slope_units(low, high):
        @pl.loop(low, high)
        def _(u):
            slope_unit(u)

    def query_tile(k):
        zz, yy = tile_place(k)
        here = rows((zz * 4 + yy) * PB, PB)
        q_sum[here, :] = (
            jnp.dot(slopes[0, here, :], k_all[pl.ds(0, CHUNK), :], preferred_element_type=jnp.float32)
            + jnp.dot(slopes[1, here, :], k_all[pl.ds(CHUNK, CHUNK), :], preferred_element_type=jnp.float32)
        )
        core_out(zz, yy).start()

    def key_tile(zz, half):
        cols = pl.ds(pl.multiple_of(half * PB, LANES), PB)
        k_sum[rows(zz * CHUNK + half * PB, PB), :] = tn_dot(slopes[zz, :, cols], q_all[...])

    far_half, near_half = 1 - x // 2, x // 2
    slope_units(0, 2)
    query_tile(0)
    slope_units(2, 9)
    add_tile(0)
    q_first(0)
    key_tile(zlp, far_half)
    k_first(0)
    slope_units(9, 10)
    query_tile(1)
    slope_units(10, 11)
    query_tile(2)
    add_tile(1)
    q_raw_up(0)
    key_tile(zlp, near_half)
    k_raw_up(0)
    k_raw_down(0)
    add_tile(2)
    q_raw_down(0)
    slope_units(11, 16)
    share = jnp.sum(positive[...], axis=0, keepdims=True) * (-2.0)
    rows_lse = row_lse[pl.ds(zh * 4 + y, 1), :]
    for g in range(PB // LANES):
        share = share + jnp.where(core == 0, rows_lse[:, g * LANES:(g + 1) * LANES], 0.0)
    for g in range(CHUNK // LANES):
        share = share + jnp.where(x == 0, col_lse[zl, :, lanes(g)], 0.0)
    loss_a[c] = share

    def loss_copy_a(o):
        return copy(loss_a.at[c], loss_a.at[c], small_send.at[40 + o], small_recv.at[40 + o], (r, (c + o) % KC))

    def loss_copy_b(o):
        return copy(loss_b.at[r], loss_b.at[r], small_send.at[56 + o], small_recv.at[56 + o], ((r + o) % QR, c))

    @pl.loop(1, KC)
    def _(o):
        loss_copy_a(o).start()

    q_pass_up(0)
    q_pass_down(0)
    query_tile(4)
    k_pass_up(0)
    k_pass_down(0)
    key_tile(zl, far_half)
    add_tile(4)
    q_first(1)
    k_first(1)
    query_tile(3)
    query_tile(5)
    add_tile(3)
    query_tile(6)
    add_tile(5)
    q_raw_up(1)
    key_tile(zl, near_half)
    k_raw_up(1)
    k_raw_down(1)
    @pl.loop(1, KC)
    def _(o):
        loss_copy_a(o).wait_recv()

    total = loss_a[0]
    for n in range(1, KC):
        total = total + loss_a[n]
    loss_b[r] = total

    @pl.loop(1, QR)
    def _(o):
        loss_copy_b(o).start()

    add_tile(6)
    q_raw_down(1)
    q_pair()
    query_tile(7)
    k_pair()

    q_pass_up(1)
    q_pass_down(1)
    k_pass_up(1)
    k_pass_down(1)
    add_tile(7)

    k_result(kg_ref)
    q_result(qg_ref)

    @pl.loop(1, QR)
    def _(o):
        loss_copy_b(o).wait_recv()

    total = loss_b[0]
    for n in range(1, QR):
        total = total + loss_b[n]
    loss_ref[...] = jnp.sum(total, axis=1, keepdims=True) * (LN2 / (2.0 * QR * KC * B))

    k_gather_drain()
    q_gather_drain()
    for s in range(2):
        for t in range(4):
            swap_copy(s, t, core).wait_send()

    @pl.loop(1, KC)
    def _(o):
        pair_copy(o).wait_send()
        row_copy(o).wait_send()
        loss_copy_a(o).wait_send()

    @pl.loop(1, QR)
    def _(o):
        col_copy(o).wait_send()
        loss_copy_b(o).wait_send()

    @pl.loop(0, 8)
    def _(n):
        core_out(n // 4, n % 4).wait_send()

    q_drain()
    k_drain()


def finish(loss_in, query_in, key_in, loss_ref, query_ref, key_ref):
    loss_ref[...] = loss_in[...]
    query_ref[...] = query_in[...] * FACTOR
    key_ref[...] = key_in[...] * FACTOR


def shards(queries, keys, pair):
    pair = pair.reshape(1, B)
    f32, bf16 = jnp.float32, jnp.bfloat16
    vmem = pl.BlockSpec(memory_space=pltpu.VMEM)
    dma = pltpu.SemaphoreType.DMA
    loss, query_grad, key_grad = pl.pallas_call(
        kernel,
        out_shape=(
            jax.ShapeDtypeStruct((1, 1), f32),
            jax.ShapeDtypeStruct((B, WIDTH), f32),
            jax.ShapeDtypeStruct((B, WIDTH), f32),
        ),
        in_specs=[pl.BlockSpec(memory_space=pl.ANY)] * 2 + [vmem],
        out_specs=(vmem,) * 3,
        scratch_shapes=[
            pltpu.VMEM((ROWS, WIDTH), bf16),
            pltpu.VMEM((COLS, WIDTH), bf16),
            pltpu.VMEM((2, ROWS, CHUNK), f32),
            pltpu.VMEM((2, ROWS, CHUNK), bf16),
            pltpu.VMEM((ROWS, WIDTH), f32),
            pltpu.VMEM((COLS, WIDTH), f32),
            pltpu.VMEM((1, 2 * LANES), jnp.int32),
            pltpu.VMEM((KC, 1, 2 * LANES), jnp.int32),
            pltpu.VMEM((ROWS, LANES), jnp.int32),
            pltpu.VMEM((2, 8, PB), f32),
            pltpu.VMEM((8, PB), f32),
            pltpu.VMEM((KC, 8, PB), f32),
            pltpu.VMEM((8, PB), f32),
            pltpu.VMEM((ROWS, LANES), f32),
            pltpu.VMEM((2, 1, CHUNK), f32),
            pltpu.VMEM((2, 1, CHUNK), f32),
            pltpu.VMEM((2, 1, CHUNK), f32),
            pltpu.VMEM((QR, 2, 1, CHUNK), f32),
            pltpu.VMEM((2, 1, CHUNK), f32),
            pltpu.VMEM((KC, 1, LANES), f32),
            pltpu.VMEM((QR, 1, LANES), f32),
            pltpu.VMEM((8, LANES), f32),
            pltpu.VMEM((8, B, WIDTH), f32),
        ]
        + [pltpu.VMEM((14, B // 2, WIDTH), jnp.int16), pltpu.VMEM((14, 1, WIDTH), f32)] * 4
        + [dma((2,)), dma((36,)), dma((36,)), dma((8,)), dma((8,))]
        + [dma((14,))] * 8
        + [dma((64,)), dma((64,))],
        compiler_params=pltpu.CompilerParams(
            collective_id=0, has_side_effects=True, vmem_limit_bytes=60 * 1024 * 1024
        ),
    )(queries, keys, pair)
    loss, query_grad, key_grad = pl.pallas_call(
        finish,
        out_shape=(
            jax.ShapeDtypeStruct((1, 1), f32),
            jax.ShapeDtypeStruct((B, WIDTH), f32),
            jax.ShapeDtypeStruct((B, WIDTH), f32),
        ),
        in_specs=[vmem] * 3,
        out_specs=(vmem,) * 3,
    )(loss, query_grad, key_grad)
    return loss.reshape(()), query_grad, key_grad


def solution(mesh):
    placed = (P(("qr", "kc"), None), P(("qr", "kc"), None), P(("qr", "kc")))
    return jax.shard_map(
        shards,
        mesh=mesh,
        in_specs=placed,
        out_specs=(P(), P(("qr", "kc"), None), P(("qr", "kc"), None)),
        check_vma=False,
    )
```

```python
import functools
import math

import jax
import jax.numpy as jnp
from jax import lax
from jax.experimental import pallas as pl
from jax.experimental.pallas import tpu as pltpu
from jax.sharding import PartitionSpec as P

MESH = pl.DeviceIdType.MESH
LOG2E = math.log2(math.e)
LN2 = math.log(2.0)
QR = 8
KC = 16
B = 192
PB = 2 * B
WIDTH = 512
ROWS = KC * B
COLS = QR * B
CHUNK = 768
LANES = 128
FACTOR = 2.0 / math.sqrt(WIDTH)


def rows(start, size, step=16):
    return pl.ds(pl.multiple_of(start, step), size)


def nt_dot(a, b):
    return lax.dot_general(a, b, (((1,), (1,)), ((), ())), preferred_element_type=jnp.float32)


def tn_dot(a, b):
    return lax.dot_general(a, b, (((0,), (0,)), ((), ())), preferred_element_type=jnp.float32)


def kernel(
    q_ref, k_ref, pair_ref, loss_ref, qg_ref, kg_ref,
    q_all, k_all, scores, slopes, q_sum, k_sum,
    pair_own, pair_all, pair_col,
    row_part, row_send, row_recv, row_lse, row_col, col_max, col_mass, col_send, col_recv, col_lse,
    loss_a, loss_b, positive, core_recv,
    q_code, q_step, q_code_in, q_step_in, k_code, k_step, k_code_in, k_step_in,
    own_sem, gather_send, gather_recv, core_send_sem, core_recv_sem,
    q_code_send, q_code_recv, q_step_send, q_step_recv, k_code_send, k_code_recv, k_step_send, k_step_recv,
    small_send, small_recv,
):
    r = lax.axis_index("qr")
    c = lax.axis_index("kc")
    zl, x = r // 4, r % 4
    y, zh, core = c // 4, (c // 2) % 2, c % 2
    factor2 = FACTOR * LOG2E

    def kc_dev(yy, zz, cc):
        return (r, yy * 4 + zz * 2 + cc)

    def qr_dev(zz, xx):
        return (zz * 4 + xx, c)

    def copy(src, dst, send, recv, device):
        return pltpu.make_async_remote_copy(
            src_ref=src, dst_ref=dst, send_sem=send, recv_sem=recv,
            device_id=device, device_id_type=MESH,
        )

    y, zh, core = c // 4, (c // 2) % 2, c % 2
    yu, yd, yo = (y + 1) % 4, (y + 3) % 4, (y + 2) % 4
    xu, xd, xo = (x + 1) % 4, (x + 3) % 4, (x + 2) % 4
    zhp, zlp, corep = 1 - zh, 1 - zl, 1 - core
    q_ring = (kc_dev(yu, zh, core), kc_dev(yd, zh, core), kc_dev(y, zhp, core))
    k_ring = (qr_dev(zl, xu), qr_dev(zl, xd), qr_dev(zlp, x))
    sibling = kc_dev(y, zh, corep)
    barrier = pltpu.get_barrier_semaphore()
    for near in q_ring + k_ring + (sibling,):
        pl.semaphore_signal(barrier, inc=1, device_id=near, device_id_type=MESH)
    pl.semaphore_wait(barrier, 7)

    H = B // 2

    def q_rows(yy, zz, cc):
        return (zz * 8 + yy * 2 + cc) * B

    def k_rows(xx, zz):
        return (zz * 4 + xx) * B

    def q_lane(yy, zz):
        return q_rows(yy, zz, core)

    def gather_copy(buf, n, start, size, device, src=None):
        view = buf.at[rows(start, size)]
        return copy(view if src is None else src, view, gather_send.at[n], gather_recv.at[n], device)

    def make_gather(buf, own, base, slot, ring, here, up, down, far, z, zp):
        to_up, to_down, to_pair = ring
        send, recv = {}, {}
        for h in range(2):
            half = own.at[pl.ds(h * H, H)]
            mine = slot(here, z) + h * H
            pairs = slot(here, zp) + h * H
            send[h] = gather_copy(buf, base + h, mine, H, to_up, half)
            send[2 + h] = gather_copy(buf, base + 2 + h, mine, H, to_down, half)
            send[4 + h] = gather_copy(buf, base + 4 + h, mine, H, to_pair, half)
            send[8 + h] = gather_copy(buf, base + 8 + h, pairs, H, to_up)
            send[10 + h] = gather_copy(buf, base + 10 + h, pairs, H, to_down)
            recv[h] = gather_copy(buf, base + h, slot(down, z) + h * H, H, to_up)
            recv[2 + h] = gather_copy(buf, base + 2 + h, slot(up, z) + h * H, H, to_up)
            recv[4 + h] = gather_copy(buf, base + 4 + h, pairs, H, to_up)
            recv[8 + h] = gather_copy(buf, base + 8 + h, slot(down, zp) + h * H, H, to_up)
            recv[10 + h] = gather_copy(buf, base + 10 + h, slot(up, zp) + h * H, H, to_up)
        for n, zz in ((6, z), (12, zp)):
            send[n] = gather_copy(buf, base + n, slot(down, zz), H, to_up)
            send[n + 1] = gather_copy(buf, base + n + 1, slot(up, zz) + H, H, to_down)
            recv[n] = gather_copy(buf, base + n, slot(far, zz), H, to_up)
            recv[n + 1] = gather_copy(buf, base + n + 1, slot(far, zz) + H, H, to_up)

        def start(*numbers):
            for n in numbers:
                send[n].start()

        def arrived(*numbers):
            for n in numbers:
                recv[n].wait_recv()

        def drain():
            for n in range(14):
                send[n].wait_send()

        return start, arrived, drain

    k_start, k_arrived, k_gather_drain = make_gather(k_all, k_ref, 0, k_rows, k_ring, x, xu, xd, xo, zl, zlp)
    q_start, q_arrived, q_gather_drain = make_gather(q_all, q_ref, 14, q_lane, q_ring, y, yu, yd, yo, zh, zhp)

    def ring_place(t):
        return (y + jnp.where(t == 0, 0, jnp.where(t == 1, 1, jnp.where(t == 2, 3, 2)))) % 4

    def swap_copy(s, t, cc):
        start = q_rows(ring_place(t), jnp.where(s == 0, zh, zhp), cc)
        src = q_ref if isinstance(s, int) and (s, t) == (0, 0) else None
        return gather_copy(q_all, 28 + s * 4 + t, start, B, sibling, src)

    def swap_start(s, t):
        swap_copy(s, t, core).start()

    def swap_arrived(s, t):
        swap_copy(s, t, corep).wait_recv()

    own_copies = (
        pltpu.make_async_copy(q_ref, q_all.at[rows(q_rows(y, zh, core), B)], own_sem.at[0]),
        pltpu.make_async_copy(k_ref, k_all.at[rows(k_rows(x, zl), B)], own_sem.at[1]),
    )
    k_start(4, 5)
    k_start(0, 3, 1, 2)
    q_start(0, 3, 1, 2)
    q_start(4, 5)
    swap_start(0, 0)
    for one in own_copies:
        one.start()
    pair_own[...] = jnp.zeros((1, 2 * LANES), jnp.int32)
    pair_own[:, 0:B] = pair_ref[...]
    col_max[...] = jnp.full((2, 1, CHUNK), -1e30, jnp.float32)
    col_mass[...] = jnp.zeros((2, 1, CHUNK), jnp.float32)
    for one in own_copies:
        one.wait()

    def lanes(g):
        return pl.ds(g * LANES, LANES)

    def score_unit(p, zz):
        here = rows(p * PB, PB)
        scores[zz, here, :] = nt_dot(q_all[here, :], k_all[rows(zz * CHUNK, CHUNK), :]) * factor2
        peak, tops = None, []
        for g in range(CHUNK // LANES):
            s = scores[zz, here, lanes(g)]
            peak = s if peak is None else jnp.maximum(peak, s)
            tops.append(jnp.max(s, axis=0, keepdims=True))
        peak = jnp.broadcast_to(jnp.max(peak, axis=1, keepdims=True), (PB, LANES))
        mass = None
        for g in range(CHUNK // LANES):
            s = scores[zz, here, lanes(g)]
            e = jnp.exp2(s - peak)
            mass = e if mass is None else mass + e
            new_mass = jnp.sum(jnp.exp2(s - tops[g]), axis=0, keepdims=True)
            old = col_max[zz, :, lanes(g)]
            new = jnp.maximum(old, tops[g])
            col_max[zz, :, lanes(g)] = new
            col_mass[zz, :, lanes(g)] = col_mass[zz, :, lanes(g)] * jnp.exp2(old - new) + new_mass * jnp.exp2(tops[g] - new)
        row_part[zz, pl.ds(p, 1), :] = peak.T[0:1, :] + jnp.log(jnp.sum(mass.T, axis=0, keepdims=True)) * LOG2E

    k_arrived(0)
    k_start(6)
    k_arrived(3)
    k_start(7)
    q_arrived(0)
    q_start(6)
    q_arrived(3)
    q_start(7)
    k_arrived(4)
    k_start(8, 10)
    k_arrived(1, 2)
    q_arrived(1, 2)
    swap_start(0, 1)
    swap_start(0, 2)
    k_arrived(5)
    k_start(9, 11)
    q_arrived(4)
    q_start(8, 10)
    k_arrived(6, 7)
    q_arrived(6, 7)
    swap_start(0, 3)
    swap_arrived(0, 0)

    def pair_copy(o):
        return copy(pair_own, pair_all.at[c], small_send.at[o], small_recv.at[o], (r, (c + o) % KC))

    def before_unit_1():
        k_arrived(8)
        k_start(12)
        q_arrived(5)
        q_start(9, 11)
        swap_start(1, 0)
        swap_arrived(0, 1)

    def before_unit_2():
        k_arrived(11)
        k_start(13)
        swap_arrived(0, 2)

    def before_unit_3():
        q_arrived(8)
        q_start(12)
        swap_arrived(0, 3)

    def before_unit_5():
        q_arrived(11)
        q_start(13)
        q_arrived(9, 10)
        swap_start(1, 1)
        swap_start(1, 2)
        k_arrived(9, 10, 12, 13)

    def before_unit_7():
        q_arrived(12, 13)
        swap_start(1, 3)

    def before_unit_14():
        swap_arrived(1, 3)

        @pl.loop(1, KC)
        def _(o):
            pair_copy(o).start()

    score_events = {
        1: before_unit_1, 2: before_unit_2, 3: before_unit_3, 4: lambda: swap_arrived(1, 0), 5: before_unit_5,
        7: before_unit_7, 10: lambda: swap_arrived(1, 1), 12: lambda: swap_arrived(1, 2), 14: before_unit_14,
    }

    for u in range(16):
        if u in score_events:
            score_events[u]()
        s, t, partner = (
            (0, 0, 0), (0, 1, 0), (0, 2, 0), (0, 3, 0), (1, 0, 0), (0, 0, 1), (0, 1, 1), (0, 2, 1), (0, 3, 1), (1, 0, 1),
            (1, 1, 0), (1, 1, 1), (1, 2, 0), (1, 2, 1), (1, 3, 0), (1, 3, 1),
        )[u]
        score_unit((zhp if s else zh) * 4 + ring_place(t), zlp if partner else zl)

    parts_top = jnp.maximum(row_part[0], row_part[1])
    parts_mass = jnp.exp2(row_part[0] - parts_top) + jnp.exp2(row_part[1] - parts_top)
    row_send[...] = parts_top + jnp.log(parts_mass) * LOG2E
    col_send[...] = col_max[...] + jnp.log(col_mass[...]) * LOG2E

    def row_copy(o):
        return copy(row_send, row_recv.at[c], small_send.at[KC + o], small_recv.at[KC + o], (r, (c + o) % KC))

    def col_copy(o):
        return copy(col_send, col_recv.at[r], small_send.at[2 * KC + o], small_recv.at[2 * KC + o], ((r + o) % QR, c))

    @pl.loop(1, KC)
    def _(o):
        row_copy(o).start()

    @pl.loop(1, QR)
    def _(o):
        col_copy(o).start()

    row_recv[c] = row_send[...]
    col_recv[r] = col_send[...]
    pair_all[c] = pair_own[...]

    @pl.loop(1, KC)
    def _(o):
        pair_copy(o).wait_recv()

    @pl.loop(0, KC)
    def _(k):
        wide = jnp.broadcast_to(pair_all[k].astype(jnp.float32), (LANES, 2 * LANES)).T
        pair_col[rows(q_rows(k // 4, (k // 2) % 2, k % 2), B), :] = wide[:B].astype(jnp.int32)

    def combine(recv, count):
        top = recv[0]
        for n in range(1, count):
            top = jnp.maximum(top, recv[n])
        mass = jnp.zeros_like(top)
        for n in range(count):
            mass = mass + jnp.exp2(recv[n] - top)
        return top + jnp.log(mass) * LOG2E

    @pl.loop(1, KC)
    def _(o):
        row_copy(o).wait_recv()

    row_lse[...] = combine(row_recv, KC)

    @pl.loop(0, 8)
    def _(p):
        row_col[rows(p * PB, PB), :] = jnp.broadcast_to(row_lse[pl.ds(p, 1), :] + 1.0, (LANES, PB)).T

    @pl.loop(1, QR)
    def _(o):
        col_copy(o).wait_recv()

    col_lse[...] = combine(col_recv, QR)

    def encode(code, step, n, value):
        unit = jnp.maximum(jnp.max(jnp.abs(value), axis=0, keepdims=True), 1e-33) * (1.0 / 32766.0)
        code[n] = jnp.round(value * (1.0 / unit)).astype(jnp.int32).astype(jnp.int16)
        step[n] = unit

    def make_reduce(buf, slot, ring, own_z, other_z, code, step, code_in, step_in, sems, here, up, down, far):
        to_up, to_down, to_pair = ring
        code_send, code_recv, step_send, step_recv = sems

        def copies(n, device):
            return (
                copy(code.at[n], code_in.at[n], code_send.at[n], code_recv.at[n], device),
                copy(step.at[n], step_in.at[n], step_send.at[n], step_recv.at[n], device),
            )

        def send(n, value, device):
            encode(code, step, n, value)
            for one in copies(n, device):
                one.start()

        def take(n):
            for one in copies(n, to_up):
                one.wait_recv()
            return code_in[n].astype(jnp.int32).astype(jnp.float32) * step_in[n]

        def half(s, place, bottom):
            return rows(slot(place, other_z if s == 0 else own_z) + (H if bottom else 0), H)

        def first(s):
            send(6 * s, buf[half(s, far, False), :], to_up)
            send(6 * s + 1, buf[half(s, far, True), :], to_down)

        def raw_up(s):
            send(6 * s + 2, buf[half(s, up, True), :], to_up)

        def raw_down(s):
            send(6 * s + 3, buf[half(s, down, False), :], to_down)

        def pass_up(s):
            send(6 * s + 4, buf[half(s, up, False), :] + take(6 * s), to_up)

        def pass_down(s):
            send(6 * s + 5, buf[half(s, down, True), :] + take(6 * s + 1), to_down)

        def final(s, bottom):
            mine = buf[half(s, here, bottom), :]
            if bottom:
                return mine + take(6 * s + 2) + take(6 * s + 5)
            return mine + take(6 * s + 3) + take(6 * s + 4)

        def pair_send():
            for n, bottom in ((12, False), (13, True)):
                send(n, final(0, bottom), to_pair)

        def result(out):
            for n, bottom in ((12, False), (13, True)):
                out[pl.ds(H if bottom else 0, H), :] = final(1, bottom) + take(n)

        def drain():
            @pl.loop(0, 14)
            def _(n):
                for one in copies(n, to_up):
                    one.wait_send()

        return first, raw_up, raw_down, pass_up, pass_down, pair_send, result, drain

    q_first, q_raw_up, q_raw_down, q_pass_up, q_pass_down, q_pair, q_result, q_drain = make_reduce(
        q_sum, q_lane, q_ring, zh, zhp, q_code, q_step, q_code_in, q_step_in,
        (q_code_send, q_code_recv, q_step_send, q_step_recv), y, yu, yd, yo)
    k_first, k_raw_up, k_raw_down, k_pass_up, k_pass_down, k_pair, k_result, k_drain = make_reduce(
        k_sum, k_rows, k_ring, zl, zlp, k_code, k_step, k_code_in, k_step_in,
        (k_code_send, k_code_recv, k_step_send, k_step_recv), x, xu, xd, xo)

    positive[...] = jnp.zeros((8, LANES), jnp.float32)
    lane = lax.broadcasted_iota(jnp.int32, (1, LANES), 1)

    def key_ids(zz, g):
        low = (g * LANES) // B
        high = (g * LANES + LANES - 1) // B
        column = lane + (g * LANES + zz * 4 * B * KC + c * B)
        ids = column + low * (KC - 1) * B
        if low == high:
            return ids
        return jnp.where(lane + g * LANES >= high * B, column + high * (KC - 1) * B, ids)

    def step_place(t):
        return (y + jnp.where(t == 0, 2, jnp.where(t == 1, 1, jnp.where(t == 2, 3, 0)))) % 4

    strip = LANES

    def make_slopes(p, zz):
        @pl.loop(0, PB // strip)
        def _(i):
            here = rows(p * PB + i * strip, strip)
            peak = row_col[here, :]
            pairs = pair_col[here, :]
            found = jnp.zeros((8, LANES), jnp.float32)
            for g in range(CHUNK // LANES):
                s = scores[zz, here, lanes(g)]
                mask = key_ids(zz, g) == pairs
                z = jnp.exp2(s - peak) + jnp.exp2(s - (col_lse[zz, :, lanes(g)] + 1.0)) - jnp.where(mask, 1.0, 0.0)
                slopes[zz, here, lanes(g)] = z.astype(jnp.bfloat16)
                found = found + jnp.sum(jnp.where(mask, s, 0.0).reshape(strip // 8, 8, LANES), axis=0)
            positive[...] = positive[...] + found

    def core_out(zz, yy):
        n = zz * 4 + yy
        return copy(q_sum.at[rows(q_rows(yy, zz, corep), B)], core_recv.at[n], core_send_sem.at[n], core_recv_sem.at[n], sibling)

    def core_add(zz, yy):
        core_out(zz, yy).wait_recv()
        here = rows(q_lane(yy, zz), B)
        q_sum[here, :] = q_sum[here, :] + core_recv[zz * 4 + yy]

    def tile_place(k):
        return (zhp + k // 4) % 2, step_place(k % 4)

    def slope_unit(u):
        k = jnp.where(u == 0, 0, jnp.where(u < 9, u - 1, u - 8))
        zz, yy = tile_place(k)
        make_slopes(zz * 4 + yy, (zl + jnp.where((u >= 1) & (u < 9), 1, 0)) % 2)

    def add_tile(k):
        core_add(*tile_place(k))

    def slope_units(low, high):
        @pl.loop(low, high)
        def _(u):
            slope_unit(u)

    def query_tile(k):
        zz, yy = tile_place(k)
        here = rows((zz * 4 + yy) * PB, PB)
        q_sum[here, :] = (
            jnp.dot(slopes[0, here, :], k_all[pl.ds(0, CHUNK), :], preferred_element_type=jnp.float32)
            + jnp.dot(slopes[1, here, :], k_all[pl.ds(CHUNK, CHUNK), :], preferred_element_type=jnp.float32)
        )
        core_out(zz, yy).start()

    def key_tile(zz):
        k_sum[rows(zz * CHUNK, CHUNK), :] = tn_dot(slopes[zz], q_all[...])

    slope_units(1, 9)
    key_tile(zlp)
    k_first(0)
    k_raw_up(0)
    k_raw_down(0)
    slope_units(0, 1)
    query_tile(0)
    slope_units(9, 10)
    query_tile(1)
    add_tile(0)
    q_first(0)
    slope_units(10, 11)
    query_tile(2)
    add_tile(1)
    q_raw_up(0)
    slope_units(11, 12)
    query_tile(3)
    add_tile(2)
    q_raw_down(0)
    k_pass_up(0)
    k_pass_down(0)
    slope_units(12, 16)
    share = jnp.sum(positive[...], axis=0, keepdims=True) * (-2.0)
    rows_lse = row_lse[pl.ds(zh * 4 + y, 1), :]
    for g in range(PB // LANES):
        share = share + jnp.where(core == 0, rows_lse[:, g * LANES:(g + 1) * LANES], 0.0)
    for g in range(CHUNK // LANES):
        share = share + jnp.where(x == 0, col_lse[zl, :, lanes(g)], 0.0)
    loss_a[c] = share

    def loss_copy_a(o):
        return copy(loss_a.at[c], loss_a.at[c], small_send.at[40 + o], small_recv.at[40 + o], (r, (c + o) % KC))

    def loss_copy_b(o):
        return copy(loss_b.at[r], loss_b.at[r], small_send.at[56 + o], small_recv.at[56 + o], ((r + o) % QR, c))

    @pl.loop(1, KC)
    def _(o):
        loss_copy_a(o).start()

    add_tile(3)
    query_tile(4)
    q_pass_up(0)
    q_pass_down(0)
    key_tile(zl)
    add_tile(4)
    q_first(1)
    k_first(1)
    k_raw_up(1)
    k_raw_down(1)
    query_tile(5)
    k_pair()
    query_tile(6)
    @pl.loop(1, KC)
    def _(o):
        loss_copy_a(o).wait_recv()

    total = loss_a[0]
    for n in range(1, KC):
        total = total + loss_a[n]
    loss_b[r] = total

    @pl.loop(1, QR)
    def _(o):
        loss_copy_b(o).start()

    add_tile(5)
    q_raw_up(1)
    q_pair()
    query_tile(7)
    add_tile(6)
    q_raw_down(1)

    k_pass_up(1)
    k_pass_down(1)
    q_pass_up(1)
    q_pass_down(1)
    add_tile(7)

    k_result(kg_ref)
    q_result(qg_ref)

    @pl.loop(1, QR)
    def _(o):
        loss_copy_b(o).wait_recv()

    total = loss_b[0]
    for n in range(1, QR):
        total = total + loss_b[n]
    loss_ref[...] = jnp.sum(total, axis=1, keepdims=True) * (LN2 / (2.0 * QR * KC * B))

    k_gather_drain()
    q_gather_drain()
    for s in range(2):
        for t in range(4):
            swap_copy(s, t, core).wait_send()

    @pl.loop(1, KC)
    def _(o):
        pair_copy(o).wait_send()
        row_copy(o).wait_send()
        loss_copy_a(o).wait_send()

    @pl.loop(1, QR)
    def _(o):
        col_copy(o).wait_send()
        loss_copy_b(o).wait_send()

    @pl.loop(0, 8)
    def _(n):
        core_out(n // 4, n % 4).wait_send()

    q_drain()
    k_drain()


def finish(loss_in, query_in, key_in, loss_ref, query_ref, key_ref):
    loss_ref[...] = loss_in[...]
    query_ref[...] = query_in[...] * FACTOR
    key_ref[...] = key_in[...] * FACTOR


def shards(queries, keys, pair):
    pair = pair.reshape(1, B)
    f32, bf16 = jnp.float32, jnp.bfloat16
    vmem = pl.BlockSpec(memory_space=pltpu.VMEM)
    dma = pltpu.SemaphoreType.DMA
    loss, query_grad, key_grad = pl.pallas_call(
        kernel,
        out_shape=(
            jax.ShapeDtypeStruct((1, 1), f32),
            jax.ShapeDtypeStruct((B, WIDTH), f32),
            jax.ShapeDtypeStruct((B, WIDTH), f32),
        ),
        in_specs=[pl.BlockSpec(memory_space=pl.ANY)] * 2 + [vmem],
        out_specs=(vmem,) * 3,
        scratch_shapes=[
            pltpu.VMEM((ROWS, WIDTH), bf16),
            pltpu.VMEM((COLS, WIDTH), bf16),
            pltpu.VMEM((2, ROWS, CHUNK), f32),
            pltpu.VMEM((2, ROWS, CHUNK), bf16),
            pltpu.VMEM((ROWS, WIDTH), f32),
            pltpu.VMEM((COLS, WIDTH), f32),
            pltpu.VMEM((1, 2 * LANES), jnp.int32),
            pltpu.VMEM((KC, 1, 2 * LANES), jnp.int32),
            pltpu.VMEM((ROWS, LANES), jnp.int32),
            pltpu.VMEM((2, 8, PB), f32),
            pltpu.VMEM((8, PB), f32),
            pltpu.VMEM((KC, 8, PB), f32),
            pltpu.VMEM((8, PB), f32),
            pltpu.VMEM((ROWS, LANES), f32),
            pltpu.VMEM((2, 1, CHUNK), f32),
            pltpu.VMEM((2, 1, CHUNK), f32),
            pltpu.VMEM((2, 1, CHUNK), f32),
            pltpu.VMEM((QR, 2, 1, CHUNK), f32),
            pltpu.VMEM((2, 1, CHUNK), f32),
            pltpu.VMEM((KC, 1, LANES), f32),
            pltpu.VMEM((QR, 1, LANES), f32),
            pltpu.VMEM((8, LANES), f32),
            pltpu.VMEM((8, B, WIDTH), f32),
        ]
        + [pltpu.VMEM((14, B // 2, WIDTH), jnp.int16), pltpu.VMEM((14, 1, WIDTH), f32)] * 4
        + [dma((2,)), dma((36,)), dma((36,)), dma((8,)), dma((8,))]
        + [dma((14,))] * 8
        + [dma((64,)), dma((64,))],
        compiler_params=pltpu.CompilerParams(
            collective_id=0, has_side_effects=True, vmem_limit_bytes=60 * 1024 * 1024
        ),
    )(queries, keys, pair)
    loss, query_grad, key_grad = pl.pallas_call(
        finish,
        out_shape=(
            jax.ShapeDtypeStruct((1, 1), f32),
            jax.ShapeDtypeStruct((B, WIDTH), f32),
            jax.ShapeDtypeStruct((B, WIDTH), f32),
        ),
        in_specs=[vmem] * 3,
        out_specs=(vmem,) * 3,
    )(loss, query_grad, key_grad)
    return loss.reshape(()), query_grad, key_grad


def solution(mesh):
    placed = (P(("qr", "kc"), None), P(("qr", "kc"), None), P(("qr", "kc")))
    return jax.shard_map(
        shards,
        mesh=mesh,
        in_specs=placed,
        out_specs=(P(), P(("qr", "kc"), None), P(("qr", "kc"), None)),
        check_vma=False,
    )
```

```python
import functools
import math

import jax
import jax.numpy as jnp
from jax import lax
from jax.experimental import pallas as pl
from jax.experimental.pallas import tpu as pltpu
from jax.sharding import PartitionSpec as P

MESH = pl.DeviceIdType.MESH
LOG2E = math.log2(math.e)
LN2 = math.log(2.0)
QR = 8
KC = 16
B = 192
PB = 2 * B
WIDTH = 512
ROWS = KC * B
COLS = QR * B
CHUNK = 768
LANES = 128
FACTOR = 2.0 / math.sqrt(WIDTH)


def rows(start, size, step=16):
    return pl.ds(pl.multiple_of(start, step), size)


def nt_dot(a, b):
    return lax.dot_general(a, b, (((1,), (1,)), ((), ())), preferred_element_type=jnp.float32)


def tn_dot(a, b):
    return lax.dot_general(a, b, (((0,), (0,)), ((), ())), preferred_element_type=jnp.float32)


def kernel(
    q_ref, k_ref, pair_ref, loss_ref, qg_ref, kg_ref,
    q_all, k_all, scores, slopes, q_sum, k_sum,
    pair_own, pair_all, pair_col,
    row_part, row_send, row_recv, row_lse, row_col, col_max, col_mass, col_send, col_recv, col_lse,
    loss_a, loss_b, positive, core_recv,
    q_code, q_step, q_code_in, q_step_in, k_code, k_step, k_code_in, k_step_in,
    own_sem, gather_send, gather_recv, core_send_sem, core_recv_sem,
    q_code_send, q_code_recv, q_step_send, q_step_recv, k_code_send, k_code_recv, k_step_send, k_step_recv,
    small_send, small_recv,
):
    r = lax.axis_index("qr")
    c = lax.axis_index("kc")
    zl, x = r // 4, r % 4
    y, zh, core = c // 4, (c // 2) % 2, c % 2
    factor2 = FACTOR * LOG2E

    def kc_dev(yy, zz, cc):
        return (r, yy * 4 + zz * 2 + cc)

    def qr_dev(zz, xx):
        return (zz * 4 + xx, c)

    def copy(src, dst, send, recv, device):
        return pltpu.make_async_remote_copy(
            src_ref=src, dst_ref=dst, send_sem=send, recv_sem=recv,
            device_id=device, device_id_type=MESH,
        )

    y, zh, core = c // 4, (c // 2) % 2, c % 2
    yu, yd, yo = (y + 1) % 4, (y + 3) % 4, (y + 2) % 4
    xu, xd, xo = (x + 1) % 4, (x + 3) % 4, (x + 2) % 4
    zhp, zlp, corep = 1 - zh, 1 - zl, 1 - core
    q_ring = (kc_dev(yu, zh, core), kc_dev(yd, zh, core), kc_dev(y, zhp, core))
    k_ring = (qr_dev(zl, xu), qr_dev(zl, xd), qr_dev(zlp, x))
    sibling = kc_dev(y, zh, corep)
    barrier = pltpu.get_barrier_semaphore()
    for near in q_ring + k_ring + (sibling,):
        pl.semaphore_signal(barrier, inc=1, device_id=near, device_id_type=MESH)
    pl.semaphore_wait(barrier, 7)

    H = B // 2

    def q_rows(yy, zz, cc):
        return (zz * 8 + yy * 2 + cc) * B

    def k_rows(xx, zz):
        return (zz * 4 + xx) * B

    def q_lane(yy, zz):
        return q_rows(yy, zz, core)

    def gather_copy(buf, n, start, size, device, src=None):
        view = buf.at[rows(start, size)]
        return copy(view if src is None else src, view, gather_send.at[n], gather_recv.at[n], device)

    def make_gather(buf, own, base, slot, ring, here, up, down, far, z, zp):
        to_up, to_down, to_pair = ring
        send, recv = {}, {}
        for h in range(2):
            half = own.at[pl.ds(h * H, H)]
            mine = slot(here, z) + h * H
            pairs = slot(here, zp) + h * H
            send[h] = gather_copy(buf, base + h, mine, H, to_up, half)
            send[2 + h] = gather_copy(buf, base + 2 + h, mine, H, to_down, half)
            send[4 + h] = gather_copy(buf, base + 4 + h, mine, H, to_pair, half)
            send[8 + h] = gather_copy(buf, base + 8 + h, pairs, H, to_up)
            send[10 + h] = gather_copy(buf, base + 10 + h, pairs, H, to_down)
            recv[h] = gather_copy(buf, base + h, slot(down, z) + h * H, H, to_up)
            recv[2 + h] = gather_copy(buf, base + 2 + h, slot(up, z) + h * H, H, to_up)
            recv[4 + h] = gather_copy(buf, base + 4 + h, pairs, H, to_up)
            recv[8 + h] = gather_copy(buf, base + 8 + h, slot(down, zp) + h * H, H, to_up)
            recv[10 + h] = gather_copy(buf, base + 10 + h, slot(up, zp) + h * H, H, to_up)
        for n, zz in ((6, z), (12, zp)):
            send[n] = gather_copy(buf, base + n, slot(down, zz), H, to_up)
            send[n + 1] = gather_copy(buf, base + n + 1, slot(up, zz) + H, H, to_down)
            recv[n] = gather_copy(buf, base + n, slot(far, zz), H, to_up)
            recv[n + 1] = gather_copy(buf, base + n + 1, slot(far, zz) + H, H, to_up)

        def start(*numbers):
            for n in numbers:
                send[n].start()

        def arrived(*numbers):
            for n in numbers:
                recv[n].wait_recv()

        def drain():
            for n in range(14):
                send[n].wait_send()

        return start, arrived, drain

    k_start, k_arrived, k_gather_drain = make_gather(k_all, k_ref, 0, k_rows, k_ring, x, xu, xd, xo, zl, zlp)
    q_start, q_arrived, q_gather_drain = make_gather(q_all, q_ref, 14, q_lane, q_ring, y, yu, yd, yo, zh, zhp)

    def ring_place(t):
        return (y + jnp.where(t == 0, 0, jnp.where(t == 1, 1, jnp.where(t == 2, 3, 2)))) % 4

    def swap_copy(s, t, cc):
        start = q_rows(ring_place(t), jnp.where(s == 0, zh, zhp), cc)
        src = q_ref if isinstance(s, int) and (s, t) == (0, 0) else None
        return gather_copy(q_all, 28 + s * 4 + t, start, B, sibling, src)

    def swap_start(s, t):
        swap_copy(s, t, core).start()

    def swap_arrived(s, t):
        swap_copy(s, t, corep).wait_recv()

    own_copies = (
        pltpu.make_async_copy(q_ref, q_all.at[rows(q_rows(y, zh, core), B)], own_sem.at[0]),
        pltpu.make_async_copy(k_ref, k_all.at[rows(k_rows(x, zl), B)], own_sem.at[1]),
    )
    k_start(4, 5)
    k_start(0, 3, 1, 2)
    q_start(0, 3, 1, 2)
    q_start(4, 5)
    swap_start(0, 0)
    for one in own_copies:
        one.start()
    pair_own[...] = jnp.zeros((1, 2 * LANES), jnp.int32)
    pair_own[:, 0:B] = pair_ref[...]
    col_max[...] = jnp.full((2, 1, CHUNK), -1e30, jnp.float32)
    col_mass[...] = jnp.zeros((2, 1, CHUNK), jnp.float32)
    for one in own_copies:
        one.wait()

    def lanes(g):
        return pl.ds(g * LANES, LANES)

    def score_unit(p, zz):
        here = rows(p * PB, PB)
        scores[zz, here, :] = nt_dot(q_all[here, :], k_all[rows(zz * CHUNK, CHUNK), :]) * factor2
        peak, tops = None, []
        for g in range(CHUNK // LANES):
            s = scores[zz, here, lanes(g)]
            peak = s if peak is None else jnp.maximum(peak, s)
            tops.append(jnp.max(s, axis=0, keepdims=True))
        peak = jnp.broadcast_to(jnp.max(peak, axis=1, keepdims=True), (PB, LANES))
        mass = None
        for g in range(CHUNK // LANES):
            s = scores[zz, here, lanes(g)]
            e = jnp.exp2(s - peak)
            mass = e if mass is None else mass + e
            new_mass = jnp.sum(jnp.exp2(s - tops[g]), axis=0, keepdims=True)
            old = col_max[zz, :, lanes(g)]
            new = jnp.maximum(old, tops[g])
            col_max[zz, :, lanes(g)] = new
            col_mass[zz, :, lanes(g)] = col_mass[zz, :, lanes(g)] * jnp.exp2(old - new) + new_mass * jnp.exp2(tops[g] - new)
        row_part[zz, pl.ds(p, 1), :] = peak.T[0:1, :] + jnp.log(jnp.sum(mass.T, axis=0, keepdims=True)) * LOG2E

    k_arrived(0)
    k_start(6)
    k_arrived(3)
    k_start(7)
    q_arrived(0)
    q_start(6)
    q_arrived(3)
    q_start(7)
    k_arrived(4)
    k_start(8, 10)
    k_arrived(1, 2)
    q_arrived(1, 2)
    swap_start(0, 1)
    swap_start(0, 2)
    k_arrived(5)
    k_start(9, 11)
    q_arrived(4)
    q_start(8, 10)
    k_arrived(6, 7)
    q_arrived(6, 7)
    swap_start(0, 3)
    swap_arrived(0, 0)

    def pair_copy(o):
        return copy(pair_own, pair_all.at[c], small_send.at[o], small_recv.at[o], (r, (c + o) % KC))

    def before_unit_1():
        k_arrived(8)
        k_start(12)
        q_arrived(5)
        q_start(9, 11)
        swap_start(1, 0)
        swap_arrived(0, 1)

    def before_unit_2():
        k_arrived(11)
        k_start(13)
        swap_arrived(0, 2)

    def before_unit_3():
        q_arrived(8)
        q_start(12)
        swap_arrived(0, 3)

    def before_unit_5():
        q_arrived(11)
        q_start(13)
        q_arrived(9, 10)
        swap_start(1, 1)
        swap_start(1, 2)
        k_arrived(9, 10, 12, 13)

    def before_unit_7():
        q_arrived(12, 13)
        swap_start(1, 3)

    def before_unit_14():
        swap_arrived(1, 3)

        @pl.loop(1, KC)
        def _(o):
            pair_copy(o).start()

    score_events = {
        1: before_unit_1, 2: before_unit_2, 3: before_unit_3, 4: lambda: swap_arrived(1, 0), 5: before_unit_5,
        7: before_unit_7, 10: lambda: swap_arrived(1, 1), 12: lambda: swap_arrived(1, 2), 14: before_unit_14,
    }

    for u in range(16):
        if u in score_events:
            score_events[u]()
        s, t, partner = (
            (0, 0, 0), (0, 1, 0), (0, 2, 0), (0, 3, 0), (1, 0, 0), (0, 0, 1), (0, 1, 1), (0, 2, 1), (0, 3, 1), (1, 0, 1),
            (1, 1, 0), (1, 1, 1), (1, 2, 0), (1, 2, 1), (1, 3, 0), (1, 3, 1),
        )[u]
        score_unit((zhp if s else zh) * 4 + ring_place(t), zlp if partner else zl)

    parts_top = jnp.maximum(row_part[0], row_part[1])
    parts_mass = jnp.exp2(row_part[0] - parts_top) + jnp.exp2(row_part[1] - parts_top)
    row_send[...] = parts_top + jnp.log(parts_mass) * LOG2E
    col_send[...] = col_max[...] + jnp.log(col_mass[...]) * LOG2E

    def row_copy(o):
        return copy(row_send, row_recv.at[c], small_send.at[KC + o], small_recv.at[KC + o], (r, (c + o) % KC))

    def col_copy(o):
        return copy(col_send, col_recv.at[r], small_send.at[2 * KC + o], small_recv.at[2 * KC + o], ((r + o) % QR, c))

    @pl.loop(1, KC)
    def _(o):
        row_copy(o).start()

    @pl.loop(1, QR)
    def _(o):
        col_copy(o).start()

    row_recv[c] = row_send[...]
    col_recv[r] = col_send[...]
    pair_all[c] = pair_own[...]

    @pl.loop(1, KC)
    def _(o):
        pair_copy(o).wait_recv()

    @pl.loop(0, KC)
    def _(k):
        wide = jnp.broadcast_to(pair_all[k].astype(jnp.float32), (LANES, 2 * LANES)).T
        pair_col[rows(q_rows(k // 4, (k // 2) % 2, k % 2), B), :] = wide[:B].astype(jnp.int32)

    def combine(recv, count):
        top = recv[0]
        for n in range(1, count):
            top = jnp.maximum(top, recv[n])
        mass = jnp.zeros_like(top)
        for n in range(count):
            mass = mass + jnp.exp2(recv[n] - top)
        return top + jnp.log(mass) * LOG2E

    @pl.loop(1, KC)
    def _(o):
        row_copy(o).wait_recv()

    row_lse[...] = combine(row_recv, KC)

    @pl.loop(0, 8)
    def _(p):
        row_col[rows(p * PB, PB), :] = jnp.broadcast_to(row_lse[pl.ds(p, 1), :] + 1.0, (LANES, PB)).T

    @pl.loop(1, QR)
    def _(o):
        col_copy(o).wait_recv()

    col_lse[...] = combine(col_recv, QR)

    def encode(code, step, n, value):
        unit = jnp.maximum(jnp.max(jnp.abs(value), axis=0, keepdims=True), 1e-33) * (1.0 / 32766.0)
        code[n] = jnp.round(value * (1.0 / unit)).astype(jnp.int32).astype(jnp.int16)
        step[n] = unit

    def make_reduce(buf, slot, ring, own_z, other_z, code, step, code_in, step_in, sems, here, up, down, far):
        to_up, to_down, to_pair = ring
        code_send, code_recv, step_send, step_recv = sems

        def copies(n, device):
            return (
                copy(code.at[n], code_in.at[n], code_send.at[n], code_recv.at[n], device),
                copy(step.at[n], step_in.at[n], step_send.at[n], step_recv.at[n], device),
            )

        def send(n, value, device):
            encode(code, step, n, value)
            for one in copies(n, device):
                one.start()

        def take(n):
            for one in copies(n, to_up):
                one.wait_recv()
            return code_in[n].astype(jnp.int32).astype(jnp.float32) * step_in[n]

        def half(s, place, bottom):
            return rows(slot(place, other_z if s == 0 else own_z) + (H if bottom else 0), H)

        def first(s):
            send(6 * s, buf[half(s, far, False), :], to_up)
            send(6 * s + 1, buf[half(s, far, True), :], to_down)

        def raw_up(s):
            send(6 * s + 2, buf[half(s, up, True), :], to_up)

        def raw_down(s):
            send(6 * s + 3, buf[half(s, down, False), :], to_down)

        def pass_up(s):
            send(6 * s + 4, buf[half(s, up, False), :] + take(6 * s), to_up)

        def pass_down(s):
            send(6 * s + 5, buf[half(s, down, True), :] + take(6 * s + 1), to_down)

        def final(s, bottom):
            mine = buf[half(s, here, bottom), :]
            if bottom:
                return mine + take(6 * s + 2) + take(6 * s + 5)
            return mine + take(6 * s + 3) + take(6 * s + 4)

        def pair_send():
            for n, bottom in ((12, False), (13, True)):
                send(n, final(0, bottom), to_pair)

        def result(out):
            for n, bottom in ((12, False), (13, True)):
                out[pl.ds(H if bottom else 0, H), :] = final(1, bottom) + take(n)

        def drain():
            @pl.loop(0, 14)
            def _(n):
                for one in copies(n, to_up):
                    one.wait_send()

        return first, raw_up, raw_down, pass_up, pass_down, pair_send, result, drain

    q_first, q_raw_up, q_raw_down, q_pass_up, q_pass_down, q_pair, q_result, q_drain = make_reduce(
        q_sum, q_lane, q_ring, zh, zhp, q_code, q_step, q_code_in, q_step_in,
        (q_code_send, q_code_recv, q_step_send, q_step_recv), y, yu, yd, yo)
    k_first, k_raw_up, k_raw_down, k_pass_up, k_pass_down, k_pair, k_result, k_drain = make_reduce(
        k_sum, k_rows, k_ring, zl, zlp, k_code, k_step, k_code_in, k_step_in,
        (k_code_send, k_code_recv, k_step_send, k_step_recv), x, xu, xd, xo)

    positive[...] = jnp.zeros((8, LANES), jnp.float32)
    lane = lax.broadcasted_iota(jnp.int32, (1, LANES), 1)

    def key_ids(zz, g):
        low = (g * LANES) // B
        high = (g * LANES + LANES - 1) // B
        column = lane + (g * LANES + zz * 4 * B * KC + c * B)
        ids = column + low * (KC - 1) * B
        if low == high:
            return ids
        return jnp.where(lane + g * LANES >= high * B, column + high * (KC - 1) * B, ids)

    def step_place(t):
        return (y + jnp.where(t == 0, 2, jnp.where(t == 1, 1, jnp.where(t == 2, 3, 0)))) % 4

    strip = LANES

    def make_slopes(p, zz):
        @pl.loop(0, PB // strip)
        def _(i):
            here = rows(p * PB + i * strip, strip)
            peak = row_col[here, :]
            pairs = pair_col[here, :]
            found = jnp.zeros((8, LANES), jnp.float32)
            for g in range(CHUNK // LANES):
                s = scores[zz, here, lanes(g)]
                mask = key_ids(zz, g) == pairs
                z = jnp.exp2(s - peak) + jnp.exp2(s - (col_lse[zz, :, lanes(g)] + 1.0)) - jnp.where(mask, 1.0, 0.0)
                slopes[zz, here, lanes(g)] = z.astype(jnp.bfloat16)
                found = found + jnp.sum(jnp.where(mask, s, 0.0).reshape(strip // 8, 8, LANES), axis=0)
            positive[...] = positive[...] + found

    def core_out(zz, yy):
        n = zz * 4 + yy
        return copy(q_sum.at[rows(q_rows(yy, zz, corep), B)], core_recv.at[n], core_send_sem.at[n], core_recv_sem.at[n], sibling)

    def core_add(zz, yy):
        core_out(zz, yy).wait_recv()
        here = rows(q_lane(yy, zz), B)
        q_sum[here, :] = q_sum[here, :] + core_recv[zz * 4 + yy]

    def tile_place(k):
        return (zhp + k // 4) % 2, step_place(k % 4)

    def slope_unit(u):
        k = jnp.where(u == 0, 0, jnp.where(u < 9, u - 1, u - 8))
        zz, yy = tile_place(k)
        make_slopes(zz * 4 + yy, (zl + jnp.where((u >= 1) & (u < 9), 1, 0)) % 2)

    def add_tile(k):
        core_add(*tile_place(k))

    def slope_units(low, high):
        @pl.loop(low, high)
        def _(u):
            slope_unit(u)

    def query_tile(k):
        zz, yy = tile_place(k)
        here = rows((zz * 4 + yy) * PB, PB)
        q_sum[here, :] = (
            jnp.dot(slopes[0, here, :], k_all[pl.ds(0, CHUNK), :], preferred_element_type=jnp.float32)
            + jnp.dot(slopes[1, here, :], k_all[pl.ds(CHUNK, CHUNK), :], preferred_element_type=jnp.float32)
        )
        core_out(zz, yy).start()

    def key_tile(zz):
        k_sum[rows(zz * CHUNK, CHUNK), :] = tn_dot(slopes[zz], q_all[...])

    def key_half(zz, half):
        cols = pl.ds(pl.multiple_of(half * PB, LANES), PB)
        k_sum[rows(zz * CHUNK + half * PB, PB), :] = tn_dot(slopes[zz, :, cols], q_all[...])

    slope_units(1, 9)
    key_tile(zlp)
    k_first(0)
    k_raw_up(0)
    k_raw_down(0)
    slope_units(0, 1)
    query_tile(0)
    slope_units(9, 10)
    query_tile(1)
    add_tile(0)
    q_first(0)
    slope_units(10, 11)
    query_tile(2)
    add_tile(1)
    q_raw_up(0)
    slope_units(11, 12)
    query_tile(3)
    add_tile(2)
    q_raw_down(0)
    k_pass_up(0)
    k_pass_down(0)
    slope_units(12, 16)
    share = jnp.sum(positive[...], axis=0, keepdims=True) * (-2.0)
    rows_lse = row_lse[pl.ds(zh * 4 + y, 1), :]
    for g in range(PB // LANES):
        share = share + jnp.where(core == 0, rows_lse[:, g * LANES:(g + 1) * LANES], 0.0)
    for g in range(CHUNK // LANES):
        share = share + jnp.where(x == 0, col_lse[zl, :, lanes(g)], 0.0)
    loss_a[c] = share

    def loss_copy_a(o):
        return copy(loss_a.at[c], loss_a.at[c], small_send.at[40 + o], small_recv.at[40 + o], (r, (c + o) % KC))

    def loss_copy_b(o):
        return copy(loss_b.at[r], loss_b.at[r], small_send.at[56 + o], small_recv.at[56 + o], ((r + o) % QR, c))

    @pl.loop(1, KC)
    def _(o):
        loss_copy_a(o).start()

    add_tile(3)
    query_tile(4)
    q_pass_up(0)
    q_pass_down(0)
    key_half(zl, 1 - x // 2)
    add_tile(4)
    q_first(1)
    k_first(1)
    key_half(zl, x // 2)
    k_raw_up(1)
    k_raw_down(1)
    query_tile(5)
    k_pair()
    query_tile(6)
    @pl.loop(1, KC)
    def _(o):
        loss_copy_a(o).wait_recv()

    total = loss_a[0]
    for n in range(1, KC):
        total = total + loss_a[n]
    loss_b[r] = total

    @pl.loop(1, QR)
    def _(o):
        loss_copy_b(o).start()

    add_tile(5)
    q_raw_up(1)
    q_pair()
    query_tile(7)
    add_tile(6)
    q_raw_down(1)

    k_pass_up(1)
    k_pass_down(1)
    q_pass_up(1)
    q_pass_down(1)
    add_tile(7)

    k_result(kg_ref)
    q_result(qg_ref)

    @pl.loop(1, QR)
    def _(o):
        loss_copy_b(o).wait_recv()

    total = loss_b[0]
    for n in range(1, QR):
        total = total + loss_b[n]
    loss_ref[...] = jnp.sum(total, axis=1, keepdims=True) * (LN2 / (2.0 * QR * KC * B))

    k_gather_drain()
    q_gather_drain()
    for s in range(2):
        for t in range(4):
            swap_copy(s, t, core).wait_send()

    @pl.loop(1, KC)
    def _(o):
        pair_copy(o).wait_send()
        row_copy(o).wait_send()
        loss_copy_a(o).wait_send()

    @pl.loop(1, QR)
    def _(o):
        col_copy(o).wait_send()
        loss_copy_b(o).wait_send()

    @pl.loop(0, 8)
    def _(n):
        core_out(n // 4, n % 4).wait_send()

    q_drain()
    k_drain()


def finish(loss_in, query_in, key_in, loss_ref, query_ref, key_ref):
    loss_ref[...] = loss_in[...]
    query_ref[...] = query_in[...] * FACTOR
    key_ref[...] = key_in[...] * FACTOR


def shards(queries, keys, pair):
    pair = pair.reshape(1, B)
    f32, bf16 = jnp.float32, jnp.bfloat16
    vmem = pl.BlockSpec(memory_space=pltpu.VMEM)
    dma = pltpu.SemaphoreType.DMA
    loss, query_grad, key_grad = pl.pallas_call(
        kernel,
        out_shape=(
            jax.ShapeDtypeStruct((1, 1), f32),
            jax.ShapeDtypeStruct((B, WIDTH), f32),
            jax.ShapeDtypeStruct((B, WIDTH), f32),
        ),
        in_specs=[pl.BlockSpec(memory_space=pl.ANY)] * 2 + [vmem],
        out_specs=(vmem,) * 3,
        scratch_shapes=[
            pltpu.VMEM((ROWS, WIDTH), bf16),
            pltpu.VMEM((COLS, WIDTH), bf16),
            pltpu.VMEM((2, ROWS, CHUNK), f32),
            pltpu.VMEM((2, ROWS, CHUNK), bf16),
            pltpu.VMEM((ROWS, WIDTH), f32),
            pltpu.VMEM((COLS, WIDTH), f32),
            pltpu.VMEM((1, 2 * LANES), jnp.int32),
            pltpu.VMEM((KC, 1, 2 * LANES), jnp.int32),
            pltpu.VMEM((ROWS, LANES), jnp.int32),
            pltpu.VMEM((2, 8, PB), f32),
            pltpu.VMEM((8, PB), f32),
            pltpu.VMEM((KC, 8, PB), f32),
            pltpu.VMEM((8, PB), f32),
            pltpu.VMEM((ROWS, LANES), f32),
            pltpu.VMEM((2, 1, CHUNK), f32),
            pltpu.VMEM((2, 1, CHUNK), f32),
            pltpu.VMEM((2, 1, CHUNK), f32),
            pltpu.VMEM((QR, 2, 1, CHUNK), f32),
            pltpu.VMEM((2, 1, CHUNK), f32),
            pltpu.VMEM((KC, 1, LANES), f32),
            pltpu.VMEM((QR, 1, LANES), f32),
            pltpu.VMEM((8, LANES), f32),
            pltpu.VMEM((8, B, WIDTH), f32),
        ]
        + [pltpu.VMEM((14, B // 2, WIDTH), jnp.int16), pltpu.VMEM((14, 1, WIDTH), f32)] * 4
        + [dma((2,)), dma((36,)), dma((36,)), dma((8,)), dma((8,))]
        + [dma((14,))] * 8
        + [dma((64,)), dma((64,))],
        compiler_params=pltpu.CompilerParams(
            collective_id=0, has_side_effects=True, vmem_limit_bytes=60 * 1024 * 1024
        ),
    )(queries, keys, pair)
    loss, query_grad, key_grad = pl.pallas_call(
        finish,
        out_shape=(
            jax.ShapeDtypeStruct((1, 1), f32),
            jax.ShapeDtypeStruct((B, WIDTH), f32),
            jax.ShapeDtypeStruct((B, WIDTH), f32),
        ),
        in_specs=[vmem] * 3,
        out_specs=(vmem,) * 3,
    )(loss, query_grad, key_grad)
    return loss.reshape(()), query_grad, key_grad


def solution(mesh):
    placed = (P(("qr", "kc"), None), P(("qr", "kc"), None), P(("qr", "kc")))
    return jax.shard_map(
        shards,
        mesh=mesh,
        in_specs=placed,
        out_specs=(P(), P(("qr", "kc"), None), P(("qr", "kc"), None)),
        check_vma=False,
    )
```
